32 devices in a mesh: dp: 8 (over z, x), tensor: 4 (over y, core).
Axes of the slice: x: 2, y: 2, z: 4, core: 2. Of those that a mesh axis runs over, the one named last changes fastest.
Arguments:
- tokens: bfloat16 [24576, 768], P('dp'), may hold values from -6 to 6
- lengths: int32 [24], P('dp'), may hold values from 64 to 1024, as said below
- first_gain: bfloat16 [768], replicated, may hold values from 0.5 to 1.5
- first_shift: bfloat16 [768], replicated, may hold values from -1.75 to 1.75
- input_weight: bfloat16 [768, 3, 768], P(None, None, 'tensor'), may hold values from -0.3125 to 0.3125
- query_value_bias: bfloat16 [2, 768], P(None, 'tensor'), may hold values from -3 to 3
- output_weight: bfloat16 [768, 768], P('tensor'), may hold values from -4 to 4
- output_bias: bfloat16 [768], replicated, may hold values from -6 to 6
- second_gain: bfloat16 [768], replicated, may hold values from 0.5 to 1.5
- second_shift: bfloat16 [768], replicated, may hold values from -1.75 to 1.75
- expand_weight: bfloat16 [768, 3072], P(None, 'tensor'), may hold values from -0.21875 to 0.21875
- expand_bias: bfloat16 [3072], P('tensor'), may hold values from -3 to 3
- reduce_weight: bfloat16 [3072, 768], P('tensor'), may hold values from -0.875 to 0.875
- reduce_bias: bfloat16 [768], replicated, may hold values from -6 to 6
- cotangent: bfloat16 [24576, 768], P('dp'), may hold values from -8 to 8
Outputs:
- block_out: bfloat16 [24576, 768], P('dp')
- tokens_grad: bfloat16 [24576, 768], P('dp')
- first_gain_grad: float32 [768], replicated
- first_shift_grad: float32 [768], replicated
- input_weight_grad: float32 [768, 3, 768], P('dp', None, 'tensor')
- query_value_bias_grad: float32 [2, 768], P(None, 'tensor')
- output_weight_grad: float32 [768, 768], P('tensor', 'dp')
- output_bias_grad: float32 [768], replicated
- second_gain_grad: float32 [768], replicated
- second_shift_grad: float32 [768], replicated
- expand_weight_grad: float32 [768, 3072], P('dp', 'tensor')
- expand_bias_grad: float32 [3072], P('tensor')
- reduce_weight_grad: float32 [3072, 768], P('tensor', 'dp')
- reduce_bias_grad: float32 [768], replicated
The draws below stay inside these ranges and needn't reach their ends.
Inputs may be any that keep to these rules, and one draw needn't show every extreme that they name: lengths[s] is the true length of sequence s; rows from lengths[s] to 1023 of its bucket are padding; some sequence has exactly 1024 and some exactly 64.
All inputs are finite; a program needn't handle non-finite values.
Results may differ from the reference program's by a relative error of at most 0.02.
The reference program's roundings to bfloat16 on the way count: a program that leaves them out, or rounds other values in their place, can miss the bound.
Values may be sent and summed in bfloat16 or wider, within the bound.
A program may use at most 192 MiB of HBM per device.

```python
import math
import jax
import jax.numpy as jnp
from jax import lax

D = 768
HD = 64
FF = 3072
SEQ = 1024
MIN_LEN = 64
SEQS = 24
TOKENS = 24576
N_TENSOR = 4


def draw_lengths(key, part):
    first, second, third = jax.random.split(key, 3)
    values = jax.random.randint(first, (SEQS,), MIN_LEN, SEQ + 1)
    longest = jax.random.randint(second, (), 0, SEQS)
    shortest = (longest + 1 + jax.random.randint(third, (), 0, SEQS - 1)) % SEQS
    values = values.at[longest].set(SEQ).at[shortest].set(MIN_LEN)
    return values.astype(jnp.int32)


def spiked(values, rng, source, target, parts, factor):
    owner, partner = [(jnp.arange(values.shape[dim]) // (values.shape[dim] // parts)).reshape([-1 if axis == dim else 1 for axis in range(values.ndim)]) for dim in (source, target)]
    chosen = jax.random.permutation(rng, parts)[partner]
    strong = (owner == chosen) | (owner == (partner + parts // 2) % parts)
    return jnp.where(strong, factor * values, values)


def levels(stream_key, dims, pieces, low, top_value):
    factor_of = 1.0
    for dim, parts in pieces:
        draws = jax.random.uniform(jax.random.fold_in(jax.random.fold_in(stream_key, 6), dim), (parts,), jnp.float32, low / len(pieces), top_value / len(pieces))
        factor_of = factor_of * jnp.repeat(jnp.exp(draws), dims[dim] // parts).reshape((-1,) + (1,) * (len(dims) - 1 - dim))
    return factor_of


def noise(stream_key, shape, width, limit, cuts=(), held_as=jnp.bfloat16):
    level = levels(stream_key, shape, cuts, -0.22, 0.18) if cuts else 1.0
    values = jax.random.normal(stream_key, shape, jnp.float32) * width * level
    return jnp.minimum(jnp.maximum(values, -limit), limit).astype(held_as)


def noise_with(key, shape, width, most, shards, heavy, kind=jnp.bfloat16):
    values = width * jax.random.normal(key, shape, jnp.float32)
    if shards:
        values = values * levels(key, shape, shards, -0.22, 0.18)
    return jnp.clip(spiked(values, jax.random.fold_in(key, 3), *heavy), -most, most).astype(kind)


def setup_inputs(seed: int = 0) -> dict:
    key_list = jax.random.split(jax.random.key(seed), 16)
    tokens = noise(key_list[0], (TOKENS, D), 1.0, 6.0, ((0, 8),))
    lengths = draw_lengths(jax.random.fold_in(key_list[15], 71), 0)
    first_gain = jnp.clip(1.0 + 0.1 * jax.random.normal(key_list[2], (D,), jnp.float32), 0.5, 1.5).astype(jnp.bfloat16)
    first_shift = noise(key_list[3], (D,), 0.3, 1.75)
    input_weight = noise(key_list[4], (D, 3, D), (D // 2) ** -0.5, 0.3125, ((2, 4),))
    query_value_bias = noise(key_list[5], (2, D), 0.5, 3.0, ((1, 4),))
    output_weight = noise(key_list[6], (D, D), 0.7, 4.0, ((0, 4),))
    output_bias = noise(key_list[7], (D,), 1.0, 6.0)
    second_gain = jnp.clip(1.0 + 0.1 * jax.random.normal(key_list[8], (D,), jnp.float32), 0.5, 1.5).astype(jnp.bfloat16)
    second_shift = noise(key_list[9], (D,), 0.3, 1.75)
    expand_weight = noise(key_list[10], (D, FF), D ** -0.5, 0.21875, ((1, 4),))
    expand_bias = noise(key_list[11], (FF,), 0.5, 3.0, ((0, 4),))
    reduce_weight = noise(key_list[12], (FF, D), 0.15, 0.875, ((0, 4),))
    reduce_bias = noise(key_list[13], (D,), 1.0, 6.0)
    cotangent = noise_with(key_list[14], (TOKENS, D), 1.0, 8.0, ((0, 8),), (0, 1, 8, 2.0))
    return {"tokens": tokens, "lengths": lengths, "first_gain": first_gain, "first_shift": first_shift, "input_weight": input_weight, "query_value_bias": query_value_bias, "output_weight": output_weight, "output_bias": output_bias, "second_gain": second_gain, "second_shift": second_shift, "expand_weight": expand_weight, "expand_bias": expand_bias, "reduce_weight": reduce_weight, "reduce_bias": reduce_bias, "cotangent": cotangent}


@jax.custom_vjp
def low(v):
    return lax.optimization_barrier(v.astype(jnp.bfloat16)).astype(jnp.float32)

@jax.custom_vjp
def low_back(v):
    return v

def low_keep(v):
    return (low(v), None)

def low_pass(kept, grad):
    return (grad,)

def back_keep(v):
    return (v, None)

def back_low(kept, grad):
    return (low(grad),)
low.defvjp(low_keep, low_pass)
low_back.defvjp(back_keep, back_low)
norm_eps = 1e-05
masked_score = -1e+30
highest = lax.Precision.HIGHEST

def norm_rows(values, gain, shift):
    centre = values - lax.optimization_barrier(jnp.mean(values, axis=-1, keepdims=True))
    spread = lax.optimization_barrier(jnp.mean(centre * centre, axis=-1, keepdims=True))
    return centre * lax.rsqrt(spread + norm_eps) * gain + shift

def attend_sequence(item):
    query, keys, values, length = item
    scores = jnp.einsum('qhd,khd->hqk', query, keys, precision=highest) * (1.0 / math.sqrt(HD))
    scores = low_back(scores)
    position = jnp.arange(SEQ)
    allowed = (position[None, :] <= position[:, None]) & (position[None, :] < length)
    scores = jnp.where(allowed[None], scores, masked_score)
    probs = jax.nn.softmax(scores, axis=-1)
    return jnp.einsum('hqk,khd->qhd', low(probs), values, precision=highest)

def forward(tokens, first_gain, first_shift, input_weight, query_value_bias, output_weight, output_bias, second_gain, second_shift, expand_weight, expand_bias, reduce_weight, reduce_bias, lengths):
    branch_scale = 1.0 / math.sqrt(24.0)
    total_rows = tokens.shape[0]
    count = lengths.shape[0]
    group = D // N_TENSOR
    heads = group // HD
    hidden_group = FF // N_TENSOR

    def shaped(values):
        return values.reshape(count, SEQ, heads, HD)
    normed = low(norm_rows(tokens, first_gain, first_shift))
    attention_total = jnp.zeros_like(tokens)
    for shard in range(N_TENSOR):
        columns = slice(shard * group, (shard + 1) * group)
        shared = low_back(normed)
        mixed = jnp.einsum('rd,djc->rjc', shared, input_weight[:, :, columns], precision=highest)
        query = low(low_back(mixed[:, 0] + query_value_bias[0, columns]))
        keys = low(low_back(mixed[:, 1]))
        values = low(low_back(mixed[:, 2] + query_value_bias[1, columns]))
        attended = lax.map(jax.checkpoint(attend_sequence), (shaped(query), shaped(keys), shaped(values), lengths))
        attended = low(low_back(attended.reshape(total_rows, group)))
        part = jnp.dot(attended, output_weight[columns], precision=highest)
        attention_total = attention_total + low(low_back(part))
    middle = tokens + branch_scale * (attention_total + output_bias)
    second = low(norm_rows(middle, second_gain, second_shift))
    feed_total = jnp.zeros_like(tokens)
    for shard in range(N_TENSOR):
        columns = slice(shard * hidden_group, (shard + 1) * hidden_group)
        shared = low_back(second)
        hidden_pre = jnp.dot(shared, expand_weight[:, columns], precision=highest) + expand_bias[columns]
        active = low(jax.nn.gelu(low_back(hidden_pre), approximate=True))
        part = jnp.dot(active, reduce_weight[columns], precision=highest)
        feed_total = feed_total + low(low_back(part))
    return middle + branch_scale * (feed_total + reduce_bias)

def reference(tokens, lengths, first_gain, first_shift, input_weight, query_value_bias, output_weight, output_bias, second_gain, second_shift, expand_weight, expand_bias, reduce_weight, reduce_bias, cotangent):
    params = [tokens, first_gain, first_shift, input_weight, query_value_bias, output_weight, output_bias, second_gain, second_shift, expand_weight, expand_bias, reduce_weight, reduce_bias]
    params = [p.astype(jnp.float32) for p in params]
    position = jnp.arange(SEQ)
    valid = (position[None, :] < lengths[:, None]).reshape(-1).astype(jnp.float32)

    def run(*inputs):
        return forward(*inputs, lengths)
    result, pull = jax.vjp(run, *params)
    grads = pull(cotangent.astype(jnp.float32) * valid[:, None])
    return (result.astype(jnp.bfloat16), grads[0].astype(jnp.bfloat16), grads[1], grads[2], grads[3], grads[4], grads[5], grads[6], grads[7], grads[8], grads[9], grads[10], grads[11], grads[12])
```

```python
import functools
import math

import jax
import jax.numpy as jnp
from jax import lax
from jax.experimental import pallas as pl
from jax.experimental.pallas import tpu as pltpu
from jax.sharding import PartitionSpec as P

MESH = pl.DeviceIdType.MESH
F32 = jnp.float32
BF = jnp.bfloat16
D = 768
W3 = 192
HD = 64
EPS = 1e-05
MASKED = -1e30
SCALE = 1.0 / math.sqrt(24.0)
VMEM_LIMIT = 65280 * 1024


def nn(a, b):
    return lax.dot_general(a, b, (((1,), (0,)), ((), ())), preferred_element_type=F32)


def nt(a, b):
    return lax.dot_general(a, b, (((1,), (1,)), ((), ())), preferred_element_type=F32)


def remote(src, dst, ssem, rsem, dev):
    return pltpu.make_async_remote_copy(
        src_ref=src, dst_ref=dst, send_sem=ssem, recv_sem=rsem, device_id=dev, device_id_type=MESH
    )


def flip(i, stride):
    return i + stride * (1 - 2 * ((i // stride) % 2))


def greet(peers):
    barrier = pltpu.get_barrier_semaphore()
    for peer in peers:
        pl.semaphore_signal(barrier, inc=1, device_id=peer, device_id_type=MESH)
    pl.semaphore_wait(barrier, len(peers))


def stats(v):
    mean = jnp.mean(v, axis=-1, keepdims=True)
    centre = v - mean
    rstd = lax.rsqrt(jnp.mean(centre * centre, axis=-1, keepdims=True) + EPS)
    return centre * rstd, rstd


def norm_back(grad, n, rstd, gain):
    e = grad * gain
    return rstd * (
        e - jnp.mean(e, axis=-1, keepdims=True) - n * jnp.mean(e * n, axis=-1, keepdims=True)
    )


def head_lanes(tile, h):
    lane = lax.broadcasted_iota(jnp.int32, tile.shape, 1)
    keep = (lane < HD) if h % 2 == 0 else (lane >= HD)
    return jnp.where(keep, tile, jnp.zeros_like(tile))


def head_tile(x, h):
    return x[:, :128] if h < 2 else x[:, 128:192]


def gelu_both(v):
    c = math.sqrt(2.0 / math.pi)
    sq = v * v
    t = jnp.tanh(c * v * (1.0 + 0.044715 * sq))
    half = 0.5 * (1.0 + t)
    slope = half + (0.5 * c) * v * (1.0 - t * t) * (1.0 + (3.0 * 0.044715) * sq)
    return v * half, slope


def kernel_one(
    len_ref, tok, cot, win, wo, wexp, wred, vec, svec,
    block_out, qkv_out, lse_out, att_out, do_out, gm_out, winr_out, ab_out, cg_out, sva,
    TOK, COT0, COT1, WIN, WO, WEXP, WRED, SV, NRM, QS, KS, VS, VT, AF, MID, SEC, SECT, GL, GLT, GL1T,
    ACT, GH, GSR, FP, FPR, GAS0, GAS1, EBA, ABS, ssem, rsem, lsem,
):
    dp = lax.axis_index("dp")
    t = lax.axis_index("tensor")
    y = t // 2
    c = t % 2
    PY = (dp, 2 * (1 - y) + c)
    PC = (dp, 2 * y + 1 - c)
    PX = (flip(dp, 1), t)
    PZ = (flip(dp, 2), t)
    bx = dp % 2
    bz = (dp // 2) % 2

    def rc(i, src, dst, dev):
        return remote(src, dst, ssem.at[i], rsem.at[i], dev)

    def lc(i, src, dst):
        return pltpu.make_async_copy(src, dst, lsem.at[i])

    class Spread:
        def __init__(self, base, src, full, rows, first):
            self.base, self.src, self.full, self.rows, self.first = base, src, full, rows // 4, first

        def part(self, ref, quarter, start=0, size=None):
            return ref.at[pl.ds(pl.multiple_of(quarter * self.rows + start, 16), size or self.rows)]

        def copy(self, kind):
            q, qx, qz = 2 * bx + bz, 2 * (1 - bx) + bz, 2 * bx + 1 - bz
            f, s = self.first, self.rows - self.first
            i = self.base + "yxzab".index(kind)
            if kind == "y":
                return rc(i, self.part(self.src, q), self.part(self.full, q), PY)
            if kind in "xz":
                return rc(
                    i, self.part(self.full, q), self.part(self.full, q), PX if kind == "x" else PZ
                )
            if kind == "a":
                return rc(i, self.part(self.full, qz, 0, f), self.part(self.full, qz, 0, f), PX)
            return rc(i, self.part(self.full, qx, f, s), self.part(self.full, qx, f, s), PZ)

        def begin(self):
            self.copy("y").start()

        def pass_on(self):
            self.copy("y").wait_recv()
            self.copy("x").start()
            self.copy("z").start()

        def pass_again(self):
            self.copy("x").wait_recv()
            self.copy("z").wait_recv()
            self.copy("a").start()
            self.copy("b").start()

        def ready(self):
            self.copy("a").wait_recv()
            self.copy("b").wait_recv()

        def close(self):
            for kind in "yxzab":
                self.copy(kind).wait_send()

    m_in = Spread(0, win, WIN.at[1], 3 * W3, 80)
    m_wo = Spread(5, wo, WO.at[1], W3, 32)
    m_exp = Spread(10, wexp, WEXP.at[1], D, 96)
    m_red = Spread(15, wred, WRED.at[1], D, 96)
    I_SV, I_WO1, I_WO2, I_E1, I_E7 = 20, 21, 22, 23, 24
    I_E2, I_E3, I_E4, I_E5, I_E6, I_EF = 25, 28, 31, 34, 37, 40

    ld_tok = [lc(0, tok.at[pl.ds(4, 4)], TOK.at[0]), lc(1, tok.at[pl.ds(8 * y, 4)], TOK.at[1])]
    ld_win = lc(2, win, WIN.at[0])
    ld_rest = [
        lc(3, wo, WO.at[0]),
        lc(4, wexp, WEXP.at[0]),
        lc(5, wred, WRED.at[0]),
        lc(6, cot.at[pl.ds(4, 4), y], COT0),
        lc(7, cot.at[pl.ds(8 * y, 4)], COT1),
    ]
    ld_tok[0].start()
    ld_win.start()
    SV[0] = svec[...]

    greet([PY, PC, PX, PZ])
    c_sv = rc(I_SV, SV.at[0], SV.at[1], PY)
    c_sv.start()
    m_in.begin()
    m_wo.begin()
    c_wo1 = rc(I_WO1, wo, WO.at[2], PC)
    c_wo1.start()
    ld_tok[1].start()
    for k in ld_rest:
        k.start()
    sva[...] = jnp.zeros_like(sva)
    EBA[...] = jnp.zeros_like(EBA)

    gain1, shift1 = vec[0:1, :], vec[1:2, :]
    obias, gain2, shift2, rbias = vec[2:3, :], vec[3:4, :], vec[4:5, :], vec[5:6, :]

    c_e1 = rc(I_E1, AF.at[0, 3], AF.at[1, 0], PY)

    def c_e2(b):
        return rc(I_E2 + b, AF.at[pl.ds(0, 2), b], AF.at[pl.ds(2, 2), b], PC)

    row_k = lax.broadcasted_iota(jnp.int32, (256, 256), 0)
    col_q = lax.broadcasted_iota(jnp.int32, (256, 256), 1)

    def save_unit(u):
        return [
            lc(8 + j + 26 * (u % 2), ref.at[u % 2], qkv_out.at[u, j])
            for j, ref in enumerate((QS, KS, VS))
        ]

    def unit(u, carry):
        nz = (u + 1) // 2
        w = u // 2
        length = len_ref[(1 - nz) + nz * 2 * y]

        @pl.when(u == 0)
        def _():
            ld_tok[0].wait()

        @pl.when(u == 1)
        def _():
            ld_tok[1].wait()

        @pl.when(u < 2)
        def _():
            for i in range(4):
                n, _ = stats(TOK[u, i].reshape(256, D).astype(F32))
                NRM[i] = (n * gain1 + shift1).astype(BF)

        @pl.when(u == 0)
        def _():
            ld_win.wait()

        @pl.when(u == 2)
        def _():
            for k in save_unit(0):
                k.wait()
            m_in.ready()
            c_sv.wait_recv()

        for i in range(4):
            x = NRM[i]
            q = nt(x, WIN[w, 0:W3, :]) + SV[w, 1:2, 0:W3]
            QS[u % 2, i] = q.astype(BF) * jnp.asarray(0.125, BF)
            k = nt(x, WIN[w, W3 : 2 * W3, :])
            KS[u % 2, i] = k.astype(BF)
            v = nt(x, WIN[w, 2 * W3 : 3 * W3, :]) + SV[w, 2:3, 0:W3]
            VS[u % 2, i] = v.astype(BF)
            VT[:, i * 256 : (i + 1) * 256] = v.T.astype(BF)
        for k in save_unit(u):
            k.start()

        @pl.when(u == 1)
        def _():
            m_wo.pass_on()

        for i in range(4):
            qi = QS[u % 2, i]
            outs = []
            for h in range(3):
                qh = head_tile(qi, h)
                if h < 2:
                    qh = head_lanes(qh, h)
                parts = []
                for kb in range(i + 1):
                    s = nt(head_tile(KS[u % 2, kb], h), qh)
                    ok = (row_k + kb * 256) < length
                    if kb == i:
                        ok = ok & (row_k <= col_q)
                    parts.append(jnp.where(ok, s, MASKED))
                top = functools.reduce(
                    jnp.maximum, [jnp.max(s, axis=0, keepdims=True) for s in parts]
                )
                total = jnp.zeros_like(top)
                acc = jnp.zeros((HD, 256), F32)
                for kb, s in enumerate(parts):
                    p = jnp.exp(s - top)
                    total = total + jnp.sum(p, axis=0, keepdims=True)
                    acc = acc + nn(
                        VT[h * HD : (h + 1) * HD, kb * 256 : (kb + 1) * 256], p.astype(BF)
                    )
                outs.append(acc * (1.0 / total))
                lse_out[u, h : h + 1, i * 256 : (i + 1) * 256] = top + jnp.log(total)
            o = jnp.concatenate(outs, axis=0).T.astype(BF)
            for hh in range(2):
                blk = (1 - nz) * (3 * ((hh + y) % 2)) + nz * (1 + i // 2)
                s0 = (1 - nz) * (i // 2) + nz * (i % 2)
                s1 = (1 - nz) * (i % 2) + nz * hh
                AF[w, blk, s0, s1] = o[hh * 128 : (hh + 1) * 128]

            if i == 2:

                @pl.when(u == 1)
                def _():
                    m_in.pass_again()

                @pl.when(u == 2)
                def _():
                    m_exp.pass_again()
                    m_red.pass_on()

        @pl.when(u == 0)
        def _():
            c_e1.start()
            m_in.pass_on()
            m_exp.begin()

        @pl.when(u == 1)
        def _():
            m_wo.pass_again()
            m_exp.pass_on()
            m_red.begin()
            c_e1.wait_recv()
            c_e2(0).start()

        return carry

    lax.fori_loop(0, 3, unit, 0)
    save_att = [
        lc(30, AF.at[0, 0], att_out.at[0, :, :, y]),
        lc(31, AF.at[0, 3], att_out.at[0, :, :, 1 - y]),
        lc(32, AF.at[0, pl.ds(1, 2)], att_out.at[1]),
        lc(33, AF.at[1, pl.ds(1, 2)], att_out.at[2]),
    ]
    for k in save_att:
        k.start()
    c_e2(1).start()
    c_e2(2).start()
    m_wo.ready()
    c_wo2 = rc(I_WO2, WO.at[1], WO.at[3], PC)
    c_wo2.start()
    winr = lc(11, WIN.at[1], winr_out)
    winr.start()
    for k in ld_rest:
        k.wait()
    c_wo1.wait_recv()
    c_wo2.wait_recv()

    def tok_rows(b, r):
        if b == 0:
            v = jnp.concatenate([TOK[0, 2 * r, y], TOK[0, 2 * r + 1, y]], axis=0)
        else:
            v = TOK[1, 2 * (b - 1) + r].reshape(256, D)
        return v.astype(F32)

    for b in range(3):
        c_e2(b).wait_recv()
        for r in range(2):
            acc = None
            for p in range(4):
                part = nn(AF[p, b, r].reshape(256, W3), WO[p])
                acc = part if acc is None else acc + part
            mid = tok_rows(b, r) + SCALE * (acc + obias)
            MID[b, 2 * r : 2 * r + 2] = mid.reshape(2, 128, D)
            n, _ = stats(mid)
            sec = n * gain2 + shift2
            SEC[b, r * 256 : (r + 1) * 256, :] = sec.astype(BF)
            SECT[:, b * 512 + r * 256 : b * 512 + (r + 1) * 256] = sec.T.astype(BF)
        if b == 0:
            m_red.pass_again()
    m_exp.ready()

    def tile(n):
        return n // 3, pl.ds(pl.multiple_of((n % 3) * 256, 256), 256)

    for b in range(3):

        def hidden(n, carry, b=b):
            shard, cols = tile(n)
            h = nn(SEC[b], WEXP[shard, :, cols]) + SV[shard, 0:1, cols]
            act, slope = gelu_both(h)
            ACT[b, n] = act.astype(BF)
            GH[b, n] = slope.astype(BF)
            return carry

        lax.fori_loop(0, 6, hidden, 0)
    m_red.ready()

    ridx = lax.broadcasted_iota(jnp.int32, (256, 1), 0)

    def grad_rows(b, r):
        if b == 0:
            g = COT0[2 * r : 2 * r + 2].reshape(256, D).astype(F32)
            p = 512 * r + 256 * (ridx // 128) + 128 * y + ridx % 128
            length = len_ref[1]
        else:
            g = COT1[2 * (b - 1) + r].reshape(256, D).astype(F32)
            p = 512 * (b - 1) + 256 * r + ridx
            length = len_ref[2 * y]
        return jnp.where(p < length, g, 0.0)

    def c_e3(b):
        return rc(I_E3 + b, SEC.at[b], GSR.at[b], PC)

    def c_e4(b):
        return rc(I_E4 + b, FP.at[b, pl.ds(2 * (1 - c), 2)], FPR.at[b, 0], PC)

    def feed_back(b):
        for r in range(2):
            g = SCALE * grad_rows(b, r)
            sva[5:6, :] += jnp.sum(g, axis=0, keepdims=True)
            GL[r * 256 : (r + 1) * 256, :] = g.astype(BF)
            GLT[:, b * 512 + r * 256 : b * 512 + (r + 1) * 256] = g.T.astype(BF)

        def active(n, carry):
            shard, rows = tile(n)
            g = nt(GL[...], WRED[shard, rows, :])
            g = (g * GH[b, n].astype(F32)).astype(BF)
            GH[b, n] = g
            EBA[n] += jnp.sum(g.astype(F32), axis=0, keepdims=True)
            return carry

        lax.fori_loop(0, 6, active, 0)

        def second(m, carry):
            rows = pl.ds(pl.multiple_of(m * 256, 256), 256)
            acc = None
            for n in range(6):
                part = nt(GH[b, n], WEXP[n // 3, rows, (n % 3) * 256 : (n % 3 + 1) * 256])
                acc = part if acc is None else acc + part
            SEC[b, :, rows] = acc.astype(BF)
            return carry

        lax.fori_loop(0, 3, second, 0)
        c_e3(b).start()

        def feed(m, carry):
            cols = pl.ds(pl.multiple_of(m * 256, 256), 256)
            acc = None
            for n in range(6):
                part = nn(ACT[b, n], WRED[n // 3, (n % 3) * 256 : (n % 3 + 1) * 256, cols])
                acc = part if acc is None else acc + part
            FP[b, :, :, cols] = acc.astype(BF).reshape(4, 128, 256)
            return carry

        lax.fori_loop(0, 3, feed, 0)
        c_e4(b).start()

    def out_rows(b, yy, cc):
        if b == 0:
            return block_out.at[pl.ds(4 + 2 * cc, 2), yy]
        return block_out.at[pl.ds(8 * yy + 2 * (b - 1) + cc, 1)]

    def bo_src(b):
        return FPR.at[0, 0] if b == 0 else FPR.at[b]

    def c_e5(b):
        return rc(I_E5 + b, bo_src(b), out_rows(b, y, c), PY)

    def c_e6(b):
        return rc(I_E6 + b, bo_src(b), out_rows(b, y, c), PC)

    def c_ef(b):
        return rc(I_EF + b, out_rows(b, 1 - y, c), out_rows(b, 1 - y, c), PC)

    def l_bo(b):
        return lc(12 + b, bo_src(b), out_rows(b, y, c))

    def finish_out(b):
        c_e4(b).wait_recv()
        two = pl.ds(2 * c, 2)
        v = MID[b, two] + SCALE * (FP[b, two].astype(F32) + FPR[b, 0].astype(F32) + rbias)
        FPR[b, 0] = v.astype(BF)
        c_e5(b).start()
        c_e6(b).start()
        l_bo(b).start()

    c_e7 = rc(I_E7, GAS0.at[1], do_out.at[0, :, y], PY)

    def l_ga(b):
        if b == 0:
            return [lc(15, GAS0.at[0], do_out.at[0, :, y])]
        two = pl.ds(2 * (b - 1), 2)
        return [lc(15 + b, GAS1.at[b - 1, 0], do_out.at[1, two]), lc(17 + b, GAS1.at[b - 1, 1], do_out.at[2, two])]

    def l_gm(b):
        return lc(20 + b, MID.at[b], gm_out.at[b])

    def middle_back(b):
        c_e3(b).wait_recv()
        for r in range(2):
            rows = slice(r * 256, (r + 1) * 256)
            g = SEC[b, rows, :].astype(F32) + GSR[b, rows, :].astype(F32)
            n, rstd = stats(MID[b, 2 * r : 2 * r + 2].reshape(256, D))
            sva[3:4, :] += jnp.sum(g * n, axis=0, keepdims=True)
            sva[4:5, :] += jnp.sum(g, axis=0, keepdims=True)
            gm = grad_rows(b, r) + norm_back(g, n, rstd, gain2)
            MID[b, 2 * r : 2 * r + 2] = gm.reshape(2, 128, D)
            low = SCALE * gm
            sva[2:3, :] += jnp.sum(low, axis=0, keepdims=True)
            GL[rows, :] = low.astype(BF)
            GL1T[:, b * 512 + r * 256 : b * 512 + (r + 1) * 256] = low.T.astype(BF)
        l_gm(b).start()
        for p in range(2):
            ga = nt(GL[...], WO[p]).astype(BF)
            if b == 0:
                GAS0[p] = ga.reshape(4, 128, W3)
            else:
                GAS1[b - 1, p] = ga.reshape(2, 2, 128, W3)
        if b == 0:
            c_e7.start()
        for k in l_ga(b):
            k.start()

    feed_back(0)
    feed_back(1)
    finish_out(0)
    middle_back(0)
    feed_back(2)
    finish_out(1)
    middle_back(1)

    def l_ab(n, kind):
        return lc(24 + n, ABS.at[n], ab_out.at[n % 3, kind, n // 3])

    def weight_grads(kind, left, right):
        def one(n, carry):
            if kind == 1:
                l_ab(n, 0).wait()
            for m in range(2):
                acc = None
                for b in range(3):
                    part = nn(
                        left[m * 384 : (m + 1) * 384, b * 512 : (b + 1) * 512], right[b, n]
                    )
                    acc = part if acc is None else acc + part
                ABS[n, 4 * m : 4 * m + 4] = acc.astype(BF).reshape(4, 96, 256)
            l_ab(n, kind).start()
            return carry

        lax.fori_loop(0, 6, one, 0)

    weight_grads(0, SECT, GH)
    finish_out(2)
    middle_back(2)
    for b in range(3):
        c_e5(b).wait_recv()
        c_ef(b).start()
    weight_grads(1, GLT, ACT)
    for p in range(2):
        for m in range(2):
            acc = None
            for b in range(3):
                part = nn(
                    GL1T[m * 384 : (m + 1) * 384, b * 512 : (b + 1) * 512],
                    AF[p, b].reshape(512, W3),
                )
                acc = part if acc is None else acc + part
            cg_out[p, 4 * m : 4 * m + 4] = acc.astype(BF).reshape(4, 96, W3)
    for n in range(6):
        row = pl.ds(8 + (t if n < 3 else 2 * (1 - y) + c), 1)
        sva[row, (n % 3) * 256 : (n % 3 + 1) * 256] = EBA[n]

    for m in (m_in, m_wo, m_exp, m_red):
        m.close()
    for k in (c_sv, c_wo1, c_wo2, c_e1, c_e7):
        k.wait_send()
    c_e7.wait_recv()
    for b in range(3):
        for k in (c_e2(b), c_e3(b), c_e4(b), c_e5(b)):
            k.wait_send()
        c_e6(b).wait()
        c_ef(b).wait()
        l_bo(b).wait()
        l_gm(b).wait()
        for k in l_ga(b):
            k.wait()
    winr.wait()
    for k in save_att:
        k.wait()
    for u in range(1, 3):
        for k in save_unit(u):
            k.wait()
    for n in range(6):
        l_ab(n, 1).wait()


def call_one(lengths, tok, cot, win, wo, wexp, wred, vec, svec):
    any_ = pl.BlockSpec(memory_space=pl.ANY)
    vm = pl.BlockSpec(memory_space=pltpu.VMEM)
    sm = pl.BlockSpec(memory_space=pltpu.SMEM)
    S = jax.ShapeDtypeStruct
    outs = [
        (S((12, 2, 128, D), BF), any_),
        (S((3, 3, 4, 256, W3), BF), any_),
        (S((3, 8, 1024), F32), vm),
        (S((3, 2, 2, 2, 128, W3), BF), any_),
        (S((3, 4, 2, 128, W3), BF), any_),
        (S((3, 4, 128, D), F32), any_),
        (S((3 * W3, D), BF), any_),
        (S((3, 2, 2, 8, 96, 256), BF), any_),
        (S((2, 8, 96, W3), BF), vm),
        (S((16, D), F32), vm),
    ]
    V = pltpu.VMEM
    scratch = [
        V((2, 4, 2, 128, D), BF),
        V((4, 128, D), BF),
        V((4, 2, 128, D), BF),
        V((2, 3 * W3, D), BF),
        V((4, W3, D), BF),
        V((2, D, D), BF),
        V((2, D, D), BF),
        V((2, 8, D), F32),
        V((4, 256, D), BF),
        V((2, 4, 256, W3), BF),
        V((2, 4, 256, W3), BF),
        V((2, 4, 256, W3), BF),
        V((W3, 1024), BF),
        V((4, 4, 2, 2, 128, W3), BF),
        V((3, 4, 128, D), F32),
        V((3, 512, D), BF),
        V((D, 1536), BF),
        V((512, D), BF),
        V((D, 1536), BF),
        V((D, 1536), BF),
        V((3, 6, 512, 256), BF),
        V((3, 6, 512, 256), BF),
        V((3, 512, D), BF),
        V((3, 4, 128, D), BF),
        V((3, 1, 2, 128, D), BF),
        V((2, 4, 128, W3), BF),
        V((2, 2, 2, 2, 128, W3), BF),
        V((6, 1, 256), F32),
        V((6, 8, 96, 256), BF),
        pltpu.SemaphoreType.DMA((43,)),
        pltpu.SemaphoreType.DMA((43,)),
        pltpu.SemaphoreType.DMA((37,)),
    ]
    return pl.pallas_call(
        kernel_one,
        out_shape=[o for o, _ in outs],
        in_specs=[sm, any_, any_, any_, any_, any_, any_, vm, vm],
        out_specs=[s for _, s in outs],
        scratch_shapes=scratch,
        compiler_params=pltpu.CompilerParams(
            collective_id=0, has_side_effects=True, vmem_limit_bytes=VMEM_LIMIT
        ),
    )(lengths, tok, cot, win, wo, wexp, wred, vec, svec)


ORDERS = ("y012", "012y", "102y", "102y", "y012", "012y", "102y")


def set_shapes(index):
    lead = (2,) if index < 3 else ()
    tail = (96, 256) if index < 3 else (96, W3)
    axes = ["y", "2", "1", "0"]
    shapes = [lead + (2,) * 4 + tail]
    places = []
    for axis in ORDERS[index]:
        at = axes.index(axis)
        axes.pop(at)
        places.append(len(lead) + at)
        shapes.append(lead + (2,) * len(axes) + tail)
    return shapes, places


def kernel_two(
    n_dp, len_ref, tok, qkv, lse, att, do, gm, win, winr, ab, cg, vec, sva,
    tok_grad, a_out, b_out, c_out, d_out, vec_out, eb_out, qv_out,
    TOK, QS, KS, VS, AT, DO, GM, WIN, NRMT, KT, DEL, DQT, DP, QVB, GN, GNR, GNS, GNSR, SHS, SHR, TG, TGS,
    ACCW, DW, SVC, SVR, *rest,
):
    ssem, rsem, lsem = rest[-3:]
    bufs = rest[:-3]
    dp = lax.axis_index("dp")
    t = lax.axis_index("tensor")
    y = t // 2
    c = t % 2
    PY = (dp, 2 * (1 - y) + c)
    PC = (dp, 2 * y + 1 - c)
    strides = []
    s = n_dp // 2
    while s >= 1:
        strides.append(s)
        s //= 2
    dp_peers = [(flip(dp, s), t) for s in strides]
    top = {"2": 0, "1": 1, "0": 2}
    peer_of = {"y": PY, "2": dp_peers[0], "1": dp_peers[1], "0": dp_peers[2]}
    bit_of = {"y": 0, **{a: (dp // strides[k]) % 2 for a, k in top.items()}}

    def rc(i, src, dst, dev):
        return remote(src, dst, ssem.at[i], rsem.at[i], dev)

    def lc(i, src, dst):
        return pltpu.make_async_copy(src, dst, lsem.at[i])

    sets = []
    pos = 0
    for index in range(7):
        shapes, places = set_shapes(index)
        if index < 3:
            whole = ab.at[index]
        elif index == 3:
            whole = cg
        else:
            whole = DW.at[index - 4]
        sums = [whole] + [bufs[pos + k] for k in range(3)]
        recvs = [bufs[pos + 3 + k] for k in range(4)]
        pos += 7
        sets.append((shapes, places, sums, recvs))

    def pick(ref, place, k):
        return ref.at[(slice(None),) * place + (k,)]

    def set_copy(index, step):
        shapes, places, sums, recvs = sets[index]
        axis = ORDERS[index][step]
        src = pick(sums[step], places[step], 1 - bit_of[axis])
        return rc(4 * index + step, src, recvs[step], peer_of[axis])

    def keep_load(index):
        shapes, places, sums, recvs = sets[index]
        axis = ORDERS[index][0]
        return lc(20 + index, pick(sums[0], places[0], bit_of[axis]), sums[1])

    def set_step(index, step):
        shapes, places, sums, recvs = sets[index]
        axis = ORDERS[index][step]
        set_copy(index, step).wait_recv()
        in_place = index < 3 and step == 0
        if in_place:
            keep_load(index).wait()
        lead = shapes[step + 1][:-2]
        count = math.prod(lead)
        for flat in range(count):
            where = []
            left = flat
            for size in reversed(lead):
                where.append(left % size)
                left //= size
            where = tuple(reversed(where))
            if in_place:
                mine = sums[1][where]
            else:
                place = places[step]
                mine = sums[step][where[:place] + (bit_of[axis],) + where[place:]]
            v = mine.astype(F32) + recvs[step][where].astype(F32)
            if step < 3:
                sums[step + 1][where] = v.astype(BF)
            elif index < 3:
                out = (a_out, b_out)[where[0]]
                out[:, index * 256 : (index + 1) * 256] = v
            elif index == 3:
                c_out[...] = v
            else:
                d_out[index - 4] = v
        if step < 3:
            set_copy(index, step + 1).start()

    lds = [
        lc(0, tok.at[pl.ds(4, 4)], TOK.at[0]),
        lc(1, tok.at[pl.ds(8 * y, 4)], TOK.at[1]),
        lc(2, qkv.at[:, 0], QS),
        lc(3, qkv.at[:, 1], KS),
        lc(4, qkv.at[:, 2], VS),
        lc(5, att, AT),
        lc(6, do, DO),
        lc(7, win, WIN.at[0]),
        lc(8, winr, WIN.at[1]),
        lc(9, gm.at[0, c], GM.at[0]),
        lc(15, gm.at[pl.ds(1, 2), :, c], GM.at[pl.ds(1, 2)]),
    ]
    for k in lds:
        k.start()
    greet([PY, PC] + dp_peers)
    for index in range(4):
        set_copy(index, 0).start()
        if index < 3:
            keep_load(index).start()
    gain1, shift1 = vec[0:1, :], vec[1:2, :]
    SVC[0] = sva[...]
    QVB[...] = jnp.zeros_like(QVB)
    DQT[...] = jnp.zeros_like(DQT)
    for k in lds:
        k.wait()

    def normed(k, carry):
        n, _ = stats(TOK[k // 4, k % 4].reshape(256, D).astype(F32))
        cols = pl.ds(pl.multiple_of((k % 4) * 256, 256), 256)
        NRMT[k // 4, :, cols] = (n * gain1 + shift1).T.astype(BF)
        return carry

    lax.fori_loop(0, 8, normed, 0)

    def prepare(u, carry):
        for i in range(4):
            cols = slice(i * 256, (i + 1) * 256)
            KT[u, :, cols] = KS[u, i].astype(F32).T.astype(BF)
            od = AT[u, i // 2, i % 2].reshape(256, W3).astype(F32) * DO[u, i].reshape(256, W3).astype(F32)
            DEL[u, 0:3, cols] = jnp.sum(od.T.reshape(3, HD, 256), axis=1)
        return carry

    lax.fori_loop(0, 3, prepare, 0)

    row_k = lax.broadcasted_iota(jnp.int32, (256, 256), 0)
    col_q = lax.broadcasted_iota(jnp.int32, (256, 256), 1)

    def block(u, j):
        w = u // 2
        nz = (u + 1) // 2
        length = len_ref[(1 - nz) + nz * 2 * y]
        inside = (row_k + j * 256) < length
        tiles_k, tiles_v = [], []
        for h in range(3):
            lanes = slice(h * HD, (h + 1) * HD)
            kt = head_tile(KS[u, j], h)
            vt = head_tile(VS[u, j], h)
            dk = dv = None
            for i in range(j, 4):
                cols = slice(i * 256, (i + 1) * 256)
                qh = head_tile(QS[u, i], h)
                gh = head_tile(DO[u, i].reshape(256, W3), h)
                if h < 2:
                    qh, gh = head_lanes(qh, h), head_lanes(gh, h)
                p = jnp.exp(nt(kt, qh) - lse[u, h : h + 1, cols])
                ok = inside & (row_k <= col_q) if i == j else inside
                p = jnp.where(ok, p, 0.0)
                ds = (p * (nt(vt, gh) - DEL[u, h : h + 1, cols])).astype(BF)
                pb = p.astype(BF)
                a, b = nn(pb, gh), nn(ds, qh)
                dv = a if dv is None else dv + a
                dk = b if dk is None else dk + b
                DQT[u, lanes, cols] += nn(KT[u, lanes, j * 256 : (j + 1) * 256], ds)
            tiles_k.append(dk)
            tiles_v.append(dv)
        gk = jnp.concatenate([tiles_k[0] + tiles_k[1], tiles_k[2]], axis=1)
        gv = jnp.concatenate([tiles_v[0] + tiles_v[1], tiles_v[2]], axis=1)
        gq = DQT[u, :, j * 256 : (j + 1) * 256].T * 0.125
        gq, gk, gv = gq.astype(BF), gk.astype(BF), gv.astype(BF)
        DP[u, 0, j] = gq
        DP[u, 1, j] = gk
        DP[u, 2, j] = gv
        QVB[w, 0:1, 0:W3] += jnp.sum(gq.astype(F32), axis=0, keepdims=True)
        QVB[w, 0:1, 256 : 256 + W3] += jnp.sum(gv.astype(F32), axis=0, keepdims=True)

    def finish_rows(g, x, middle):
        n, rstd = stats(x.astype(F32))
        SVC[0, 0:1, :] += jnp.sum(g * n, axis=0, keepdims=True)
        SVC[0, 1:2, :] += jnp.sum(g, axis=0, keepdims=True)
        return (middle + norm_back(g, n, rstd, gain1)).astype(BF)

    for j in range(4):
        block(0, j)
    for i in range(4):
        acc = None
        for k in range(3):
            part = nn(DP[0, k, i], WIN[0, k * W3 : (k + 1) * W3, :])
            acc = part if acc is None else acc + part
        GNS[i] = acc.astype(BF).reshape(2, 128, D)
    c_core = rc(32, GNS.at[pl.ds(2 * (1 - c), 2)], GNSR, PC)
    c_core.start()
    c_y = rc(33, SHS, SHR, PY)

    def share_rows():
        c_core.wait_recv()
        for k in range(2):
            v = GNS[2 * c + k, 1 - y].astype(F32) + GNSR[k, 1 - y].astype(F32)
            SHS[k] = v.astype(BF)
        c_y.start()

    def shared_out(yy, cc):
        return tok_grad.at[pl.ds(4 + 2 * cc, 2), yy]

    t_y = rc(46, TGS, shared_out(y, c), PY)
    t_c = rc(47, TGS, shared_out(y, c), PC)
    t_f = rc(48, shared_out(1 - y, c), shared_out(1 - y, c), PC)
    t_l = lc(10, TGS, shared_out(y, c))

    def finish_shared():
        c_y.wait_recv()
        for k in range(2):
            g = GNS[2 * c + k, y].astype(F32) + GNSR[k, y].astype(F32) + SHR[k].astype(F32)
            TGS[k] = finish_rows(g, TOK[0, 2 * c + k, y], GM[0, k])
        t_y.start()
        t_c.start()
        t_l.start()

    def c_gn(j):
        return rc(28 + j, GN.at[j, 1 - c], GNR.at[j], PC)

    def own_out(j, yy, cc):
        return tok_grad.at[8 * yy + j, cc]

    def c_own(j, k):
        if k == 0:
            return rc(34 + j, TG.at[j], own_out(j, y, c), PY)
        if k == 1:
            return rc(38 + j, TG.at[j], own_out(j, y, c), PC)
        if k == 2:
            return rc(42 + j, own_out(j, 1 - y, c), own_out(j, 1 - y, c), PC)
        return lc(11 + j, TG.at[j], own_out(j, y, c))

    def rows_back(j):
        acc = None
        for w in range(2):
            for k in range(3):
                part = nn(DP[1 + w, k, j], WIN[w, k * W3 : (k + 1) * W3, :])
                acc = part if acc is None else acc + part
        GN[j] = acc.astype(BF).reshape(2, 128, D)
        c_gn(j).start()

    def finish_own(j):
        c_gn(j).wait_recv()
        g = GN[j, c].astype(F32) + GNR[j].astype(F32)
        TG[j] = finish_rows(g, TOK[1, j, c], GM[1 + j // 2, j % 2])
        for k in (0, 1, 3):
            c_own(j, k).start()

    def pass_own(j):
        c_own(j, 0).wait_recv()
        c_own(j, 2).start()

    def own_blocks(j):
        def one(u, carry):
            block(u, j)
            return carry

        lax.fori_loop(1, 3, one, 0)

    def input_grads(first):
        for k in range(3):
            for w in range(2):
                for m in range(2):
                    rows = slice(m * 384, (m + 1) * 384)
                    if first:
                        acc = nn(NRMT[1, rows, 0:768], DP[1 + w, k, 0:3].reshape(768, W3))
                        if w == 0:
                            acc = acc + nn(NRMT[0, rows, :], DP[0, k].reshape(1024, W3))
                        ACCW[w, k, rows, :] = acc
                    else:
                        acc = ACCW[w, k, rows, :] + nn(NRMT[1, rows, 768:1024], DP[1 + w, k, 3])
                        DW[k, w, m] = acc.astype(BF).reshape(2, 2, 96, W3)
            if not first:
                set_copy(4 + k, 0).start()

    own_blocks(0)
    share_rows()
    rows_back(0)
    for index in range(4):
        set_step(index, 0)
    own_blocks(1)
    finish_own(0)
    rows_back(1)
    finish_shared()
    own_blocks(2)
    pass_own(0)
    finish_own(1)
    rows_back(2)
    for index in range(4):
        set_step(index, 1)
    input_grads(True)
    finish_own(2)
    own_blocks(3)
    rows_back(3)
    input_grads(False)
    finish_own(3)
    for w in range(2):
        row = pl.ds(12 + (t if w == 0 else 2 * (1 - y) + c), 1)
        SVC[0, row, :] = QVB[w]

    peers = [PC, PY] + dp_peers

    def c_sum(k):
        return rc(49 + k, SVC.at[k], SVR.at[k], peers[k])

    def sum_step(k):
        c_sum(k).wait_recv()
        SVC[k + 1] = SVC[k] + SVR[k]
        if k + 1 < len(peers):
            c_sum(k + 1).start()

    c_sum(0).start()
    t_y.wait_recv()
    t_f.start()
    pass_own(1)
    pass_own(2)
    sum_step(0)
    for index in range(4):
        set_step(index, 2)
    sum_step(1)
    for index in range(4, 7):
        set_step(index, 0)
    pass_own(3)
    sum_step(2)
    for index in range(4):
        set_step(index, 3)
    for k in range(3, len(peers)):
        sum_step(k)
    for step in range(1, 4):
        for index in range(4, 7):
            set_step(index, step)
    last = len(peers)
    both = lax.broadcasted_iota(jnp.int32, (8, 1), 0) >= 2
    vec_out[...] = jnp.where(both, 0.5, 1.0) * SVC[last, 0:8, :]
    eb_out[...] = SVC[last, pl.ds(8 + t, 1), :]
    qv_out[...] = SVC[last, pl.ds(12 + t, 1), :]

    for index in range(7):
        for step in range(4):
            set_copy(index, step).wait_send()
    for k in range(len(peers)):
        c_sum(k).wait_send()
    for j in range(4):
        c_gn(j).wait_send()
        c_own(j, 0).wait_send()
        for k in (1, 2, 3):
            c_own(j, k).wait()
    c_core.wait_send()
    c_y.wait_send()
    t_y.wait_send()
    t_c.wait()
    t_f.wait()
    t_l.wait()


def call_two(n_dp, lengths, tok, qkv, lse, att, do, gm, win, winr, ab, cg, vec, sva):
    any_ = pl.BlockSpec(memory_space=pl.ANY)
    vm = pl.BlockSpec(memory_space=pltpu.VMEM)
    sm = pl.BlockSpec(memory_space=pltpu.SMEM)
    S = jax.ShapeDtypeStruct
    outs = [
        (S((12, 2, 128, D), BF), any_),
        (S((96, D), F32), vm),
        (S((96, D), F32), vm),
        (S((96, W3), F32), vm),
        (S((3, 96, W3), F32), vm),
        (S((8, D), F32), vm),
        (S((1, D), F32), vm),
        (S((1, D), F32), vm),
    ]
    V = pltpu.VMEM
    steps = 2 + n_dp.bit_length() - 1
    scratch = [
        V((2, 4, 2, 128, D), BF),
        V((3, 4, 256, W3), BF),
        V((3, 4, 256, W3), BF),
        V((3, 4, 256, W3), BF),
        V((3, 2, 2, 2, 128, W3), BF),
        V((3, 4, 2, 128, W3), BF),
        V((3, 2, 128, D), F32),
        V((2, 3 * W3, D), BF),
        V((2, D, 1024), BF),
        V((3, W3, 1024), BF),
        V((3, 8, 1024), F32),
        V((3, W3, 1024), F32),
        V((3, 3, 4, 256, W3), BF),
        V((2, 1, D), F32),
        V((4, 2, 128, D), BF),
        V((4, 128, D), BF),
        V((4, 2, 128, D), BF),
        V((2, 2, 128, D), BF),
        V((2, 128, D), BF),
        V((2, 128, D), BF),
        V((4, 128, D), BF),
        V((2, 128, D), BF),
        V((2, 3, D, W3), F32),
        V((3, 2, 2, 2, 2, 96, W3), BF),
        V((steps + 1, 16, D), F32),
        V((steps, 16, D), F32),
    ]
    for index in range(7):
        shapes, _ = set_shapes(index)
        scratch += [V(shapes[k], BF) for k in (1, 2, 3)] + [V(shapes[k], BF) for k in (1, 2, 3, 4)]
    scratch += [
        pltpu.SemaphoreType.DMA((49 + steps,)),
        pltpu.SemaphoreType.DMA((49 + steps,)),
        pltpu.SemaphoreType.DMA((23,)),
    ]
    return pl.pallas_call(
        functools.partial(kernel_two, n_dp),
        out_shape=[o for o, _ in outs],
        in_specs=[sm, any_, any_, vm, any_, any_, any_, any_, any_, any_, vm, vm, vm],
        out_specs=[s for _, s in outs],
        scratch_shapes=scratch,
        compiler_params=pltpu.CompilerParams(
            collective_id=1, has_side_effects=True, vmem_limit_bytes=VMEM_LIMIT
        ),
    )(lengths, tok, qkv, lse, att, do, gm, win, winr, ab, cg, vec, sva)


def body(
    n_dp, tokens, lengths, first_gain, first_shift, input_weight, query_value_bias, output_weight,
    output_bias, second_gain, second_shift, expand_weight, expand_bias, reduce_weight, reduce_bias,
    cotangent,
):
    tok = tokens.reshape(12, 2, 128, D)
    cot = cotangent.reshape(12, 2, 128, D)
    win = jnp.transpose(input_weight, (1, 2, 0)).reshape(3 * W3, D)
    zero = jnp.zeros((D,), F32)
    vec = jnp.stack(
        [
            v.astype(F32)
            for v in (first_gain, first_shift, output_bias, second_gain, second_shift, reduce_bias)
        ]
        + [zero, zero]
    )
    qv = query_value_bias.astype(F32)
    pad = jnp.zeros((D - W3,), F32)
    svec = jnp.stack(
        [
            expand_bias.astype(F32),
            jnp.concatenate([qv[0], pad]),
            jnp.concatenate([qv[1], pad]),
        ]
        + [zero] * 5
    )
    block_out, qkv, lse, att, do, gm, winr, ab, cg, sva = call_one(
        lengths, tok, cot, win, output_weight, expand_weight, reduce_weight, vec, svec
    )
    tok_grad, a, b, cc, d, rep, eb, qvg = call_two(
        n_dp, lengths, tok, qkv, lse, att, do, gm.reshape(3, 2, 2, 128, D), win, winr,
        ab.reshape(3, 2, 2, 2, 2, 2, 96, 256), cg.reshape(2, 2, 2, 2, 96, W3), vec, sva,
    )
    d = jnp.transpose(d, (1, 0, 2))
    left = n_dp // 8
    if left > 1:
        groups = [list(range(k * left, (k + 1) * left)) for k in range(8)]
        a, b, cc, d = [
            lax.psum_scatter(v, "dp", scatter_dimension=0, axis_index_groups=groups, tiled=True)
            for v in (a, b, cc, d)
        ]
    return (
        block_out.reshape(tokens.shape),
        tok_grad.reshape(tokens.shape),
        rep[0],
        rep[1],
        d,
        jnp.stack([qvg[0, 0:W3], qvg[0, 256 : 256 + W3]]),
        cc.T,
        rep[2],
        rep[3],
        rep[4],
        a,
        eb[0],
        b.T,
        rep[5],
    )


def solution(mesh):
    return jax.shard_map(
        functools.partial(body, mesh.shape["dp"]),
        mesh=mesh,
        in_specs=(
            P("dp", None),
            P("dp"),
            P(),
            P(),
            P(None, None, "tensor"),
            P(None, "tensor"),
            P("tensor", None),
            P(),
            P(),
            P(),
            P(None, "tensor"),
            P("tensor"),
            P("tensor", None),
            P(),
            P("dp", None),
        ),
        out_specs=(
            P("dp", None),
            P("dp", None),
            P(),
            P(),
            P("dp", None, "tensor"),
            P(None, "tensor"),
            P("tensor", "dp"),
            P(),
            P(),
            P(),
            P("dp", "tensor"),
            P("tensor"),
            P("tensor", "dp"),
            P(),
        ),
        check_vma=False,
    )
```

```python
import functools
import math

import jax
import jax.numpy as jnp
from jax import lax
from jax.experimental import pallas as pl
from jax.experimental.pallas import tpu as pltpu
from jax.sharding import PartitionSpec as P

MESH = pl.DeviceIdType.MESH
F32 = jnp.float32
BF = jnp.bfloat16
D = 768
W3 = 192
HD = 64
EPS = 1e-05
MASKED = -1e30
SCALE = 1.0 / math.sqrt(24.0)
VMEM_LIMIT = 65280 * 1024


def nn(a, b):
    return lax.dot_general(a, b, (((1,), (0,)), ((), ())), preferred_element_type=F32)


def nt(a, b):
    return lax.dot_general(a, b, (((1,), (1,)), ((), ())), preferred_element_type=F32)


def remote(src, dst, ssem, rsem, dev):
    return pltpu.make_async_remote_copy(
        src_ref=src, dst_ref=dst, send_sem=ssem, recv_sem=rsem, device_id=dev, device_id_type=MESH
    )


def flip(i, stride):
    return i + stride * (1 - 2 * ((i // stride) % 2))


def greet(peers):
    barrier = pltpu.get_barrier_semaphore()
    for peer in peers:
        pl.semaphore_signal(barrier, inc=1, device_id=peer, device_id_type=MESH)
    pl.semaphore_wait(barrier, len(peers))


def stats(v):
    mean = jnp.mean(v, axis=-1, keepdims=True)
    centre = v - mean
    rstd = lax.rsqrt(jnp.mean(centre * centre, axis=-1, keepdims=True) + EPS)
    return centre * rstd, rstd


def norm_back(grad, n, rstd, gain):
    e = grad * gain
    return rstd * (
        e - jnp.mean(e, axis=-1, keepdims=True) - n * jnp.mean(e * n, axis=-1, keepdims=True)
    )


def row(ref):
    return ref[...].astype(F32).reshape(1, D)


def head_lanes(tile, h):
    lane = lax.broadcasted_iota(jnp.int32, tile.shape, 1)
    keep = (lane < HD) if h % 2 == 0 else (lane >= HD)
    return jnp.where(keep, tile, jnp.zeros_like(tile))


def head_tile(x, h):
    return x[:, :128] if h < 2 else x[:, 128:192]


def gelu_both(v):
    c = math.sqrt(2.0 / math.pi)
    sq = v * v
    t = jnp.tanh(c * v * (1.0 + 0.044715 * sq))
    half = 0.5 * (1.0 + t)
    slope = half + (0.5 * c) * v * (1.0 - t * t) * (1.0 + (3.0 * 0.044715) * sq)
    return v * half, slope


def kernel_one(
    len_ref, tok, cot, win, wo, wexp, wred, g1, s1, ob, g2, s2, rb, eb, qvb,
    block_out, qkv_out, lse_out, att_out, do_out, gm_out, winr_out, ab_out, cg_out, sva,
    TOK, COT0, COT1, WIN, WO, WEXP, WRED, SV, NRM, QS, KS, VS, VT, AF, MID, SEC, SECT, GL, GLT, GL1T,
    ACT, GH, GSR, FP, FPR, GAS0, GAS1, EBA, ABS, ssem, rsem, lsem,
):
    dp = lax.axis_index("dp")
    t = lax.axis_index("tensor")
    y = t // 2
    c = t % 2
    PY = (dp, 2 * (1 - y) + c)
    PC = (dp, 2 * y + 1 - c)
    PX = (flip(dp, 1), t)
    PZ = (flip(dp, 2), t)
    bx = dp % 2
    bz = (dp // 2) % 2

    def rc(i, src, dst, dev):
        return remote(src, dst, ssem.at[i], rsem.at[i], dev)

    def lc(i, src, dst):
        return pltpu.make_async_copy(src, dst, lsem.at[i])

    class Spread:
        def __init__(self, base, src, full, rows, first):
            self.base, self.src, self.full, self.rows, self.first = base, src, full, rows // 4, first

        def part(self, ref, quarter, start=0, size=None):
            return ref.at[pl.ds(pl.multiple_of(quarter * self.rows + start, 16), size or self.rows)]

        def copy(self, kind):
            q, qx, qz = 2 * bx + bz, 2 * (1 - bx) + bz, 2 * bx + 1 - bz
            f, s = self.first, self.rows - self.first
            i = self.base + "yxzab".index(kind)
            if kind == "y":
                return rc(i, self.part(self.src, q), self.part(self.full, q), PY)
            if kind in "xz":
                return rc(
                    i, self.part(self.full, q), self.part(self.full, q), PX if kind == "x" else PZ
                )
            if kind == "a" and f == 0:
                q = 3 - q
                return rc(i, self.part(self.src, q), self.part(self.full, q), PY)
            if kind == "a":
                return rc(i, self.part(self.full, qz, 0, f), self.part(self.full, qz, 0, f), PX)
            return rc(i, self.part(self.full, qx, f, s), self.part(self.full, qx, f, s), PZ)

        def begin(self):
            self.copy("y").start()

        def pass_on(self):
            self.copy("y").wait_recv()
            self.copy("x").start()
            self.copy("z").start()
            if self.first == 0:
                self.copy("a").start()

        def pass_again(self):
            self.copy("x").wait_recv()
            self.copy("z").wait_recv()
            self.copy("a").start()
            self.copy("b").start()

        def ready(self):
            for kind in "xza" if self.first == 0 else "ab":
                self.copy(kind).wait_recv()

        def close(self):
            for kind in "yxza" if self.first == 0 else "yxzab":
                self.copy(kind).wait_send()

    m_in = Spread(0, win, WIN.at[1], 3 * W3, 0)
    m_wo = Spread(5, wo, WO.at[1], W3, 0)
    m_exp = Spread(10, wexp, WEXP.at[1], D, 96)
    m_red = Spread(15, wred, WRED.at[1], D, 96)
    I_SV, I_WO1, I_WO2, I_E1, I_E7 = 20, 21, 22, 23, 24
    I_E2, I_E3, I_E4, I_E5, I_E6, I_EF = 25, 28, 31, 34, 37, 40

    ld_tok = [lc(0, tok.at[pl.ds(4, 4)], TOK.at[0]), lc(1, tok.at[pl.ds(8 * y, 4)], TOK.at[1])]
    ld_win = lc(2, win, WIN.at[0])
    ld_rest = [
        lc(3, wo, WO.at[0]),
        lc(4, wexp, WEXP.at[0]),
        lc(5, wred, WRED.at[0]),
        lc(6, cot.at[pl.ds(4, 4), y], COT0),
        lc(7, cot.at[pl.ds(8 * y, 4)], COT1),
    ]
    ld_tok[0].start()
    ld_win.start()
    SV[0] = jnp.zeros((8, D), F32)
    SV[0, 0:1, :] = row(eb)
    SV[0, 1:3, 0:W3] = qvb[...].astype(F32)

    greet([PY, PC, PX, PZ])
    c_sv = rc(I_SV, SV.at[0], SV.at[1], PY)
    c_sv.start()
    m_in.begin()
    m_wo.begin()
    c_wo1 = rc(I_WO1, wo, WO.at[2], PC)
    c_wo1.start()
    ld_tok[1].start()
    for k in ld_rest:
        k.start()
    sva[...] = jnp.zeros_like(sva)
    EBA[...] = jnp.zeros_like(EBA)

    gain1, shift1 = row(g1), row(s1)
    obias, gain2, shift2, rbias = row(ob), row(g2), row(s2), row(rb)

    c_e1 = rc(I_E1, AF.at[0, 3], AF.at[1, 0], PY)

    def c_e2(b):
        return rc(I_E2 + b, AF.at[pl.ds(0, 2), b], AF.at[pl.ds(2, 2), b], PC)

    row_k = lax.broadcasted_iota(jnp.int32, (256, 256), 0)
    col_q = lax.broadcasted_iota(jnp.int32, (256, 256), 1)

    def save_unit(u):
        return [
            lc(8 + j + 26 * (u % 2), ref.at[u % 2], qkv_out.at[u, j])
            for j, ref in enumerate((QS, KS, VS))
        ]

    def unit(u, carry):
        nz = (u + 1) // 2
        w = u // 2
        length = len_ref[(1 - nz) + nz * 2 * y]

        @pl.when(u == 0)
        def _():
            ld_tok[0].wait()

        @pl.when(u == 1)
        def _():
            ld_tok[1].wait()

        @pl.when(u < 2)
        def _():
            for i in range(4):
                n, _ = stats(TOK[u, i].reshape(256, D).astype(F32))
                NRM[i] = (n * gain1 + shift1).astype(BF)

        @pl.when(u == 0)
        def _():
            ld_win.wait()

        @pl.when(u == 2)
        def _():
            for k in save_unit(0):
                k.wait()
            m_in.ready()
            c_sv.wait_recv()

        for i in range(4):
            x = NRM[i]
            q = nt(x, WIN[w, 0:W3, :]) + SV[w, 1:2, 0:W3]
            QS[u % 2, i] = q.astype(BF) * jnp.asarray(0.125, BF)
            k = nt(x, WIN[w, W3 : 2 * W3, :])
            KS[u % 2, i] = k.astype(BF)
            v = nt(x, WIN[w, 2 * W3 : 3 * W3, :]) + SV[w, 2:3, 0:W3]
            VS[u % 2, i] = v.astype(BF)
            VT[:, i * 256 : (i + 1) * 256] = v.T.astype(BF)
        for k in save_unit(u):
            k.start()

        for i in range(4):
            qi = QS[u % 2, i]
            outs = []
            for h in range(3):
                qh = head_tile(qi, h)
                if h < 2:
                    qh = head_lanes(qh, h)
                parts = []
                for kb in range(i + 1):
                    s = nt(head_tile(KS[u % 2, kb], h), qh)
                    ok = (row_k + kb * 256) < length
                    if kb == i:
                        ok = ok & (row_k <= col_q)
                    parts.append(jnp.where(ok, s, MASKED))
                top = functools.reduce(
                    jnp.maximum, [jnp.max(s, axis=0, keepdims=True) for s in parts]
                )
                total = jnp.zeros_like(top)
                acc = jnp.zeros((HD, 256), F32)
                for kb, s in enumerate(parts):
                    p = jnp.exp(s - top)
                    total = total + jnp.sum(p, axis=0, keepdims=True)
                    acc = acc + nn(
                        VT[h * HD : (h + 1) * HD, kb * 256 : (kb + 1) * 256], p.astype(BF)
                    )
                outs.append(acc * (1.0 / total))
                lse_out[u, h : h + 1, i * 256 : (i + 1) * 256] = top + jnp.log(total)
            o = jnp.concatenate(outs, axis=0).T.astype(BF)
            for hh in range(2):
                blk = (1 - nz) * (3 * ((hh + y) % 2)) + nz * (1 + i // 2)
                s0 = (1 - nz) * (i // 2) + nz * (i % 2)
                s1 = (1 - nz) * (i % 2) + nz * hh
                AF[w, blk, s0, s1] = o[hh * 128 : (hh + 1) * 128]

        @pl.when(u == 0)
        def _():
            c_e1.start()
            m_in.pass_on()
            m_exp.begin()

        @pl.when(u == 1)
        def _():
            m_wo.pass_on()
            m_red.begin()
            c_e1.wait_recv()
            c_e2(0).start()

        return carry

    lax.fori_loop(0, 3, unit, 0)
    save_att = [
        lc(30, AF.at[0, 0], att_out.at[0, :, :, y]),
        lc(31, AF.at[0, 3], att_out.at[0, :, :, 1 - y]),
        lc(32, AF.at[0, pl.ds(1, 2)], att_out.at[1]),
        lc(33, AF.at[1, pl.ds(1, 2)], att_out.at[2]),
    ]
    for k in save_att:
        k.start()
    c_e2(1).start()
    c_e2(2).start()
    m_exp.pass_on()
    m_wo.ready()
    c_wo2 = rc(I_WO2, WO.at[1], WO.at[3], PC)
    c_wo2.start()
    winr = lc(11, WIN.at[1], winr_out)
    winr.start()
    for k in ld_rest:
        k.wait()
    c_wo1.wait_recv()
    c_wo2.wait_recv()

    def tok_rows(b, r):
        if b == 0:
            v = jnp.concatenate([TOK[0, 2 * r, y], TOK[0, 2 * r + 1, y]], axis=0)
        else:
            v = TOK[1, 2 * (b - 1) + r].reshape(256, D)
        return v.astype(F32)

    for b in range(3):
        c_e2(b).wait_recv()
        for r in range(2):
            acc = None
            for p in range(4):
                part = nn(AF[p, b, r].reshape(256, W3), WO[p])
                acc = part if acc is None else acc + part
            mid = tok_rows(b, r) + SCALE * (acc + obias)
            MID[b, 2 * r : 2 * r + 2] = mid.reshape(2, 128, D)
            n, _ = stats(mid)
            sec = n * gain2 + shift2
            SEC[b, r * 256 : (r + 1) * 256, :] = sec.astype(BF)
            SECT[:, b * 512 + r * 256 : b * 512 + (r + 1) * 256] = sec.T.astype(BF)
        if b == 1:
            m_red.pass_on()
    m_exp.pass_again()

    def tile(n):
        return n // 3, pl.ds(pl.multiple_of((n % 3) * 256, 256), 256)

    def hidden_part(first):
        for b in range(3):

            def hidden(n, carry, b=b):
                shard, cols = tile(n)
                h = nn(SEC[b], WEXP[shard, :, cols]) + SV[shard, 0:1, cols]
                act, slope = gelu_both(h)
                ACT[b, n] = act.astype(BF)
                GH[b, n] = slope.astype(BF)
                return carry

            lax.fori_loop(first, first + 3, hidden, 0)

    hidden_part(0)
    m_red.pass_again()
    m_exp.ready()
    hidden_part(3)
    m_red.ready()

    ridx = lax.broadcasted_iota(jnp.int32, (256, 1), 0)

    def grad_rows(b, r):
        if b == 0:
            g = COT0[2 * r : 2 * r + 2].reshape(256, D).astype(F32)
            p = 512 * r + 256 * (ridx // 128) + 128 * y + ridx % 128
            length = len_ref[1]
        else:
            g = COT1[2 * (b - 1) + r].reshape(256, D).astype(F32)
            p = 512 * (b - 1) + 256 * r + ridx
            length = len_ref[2 * y]
        return jnp.where(p < length, g, 0.0)

    def c_e3(b):
        return rc(I_E3 + b, SEC.at[b], GSR.at[b], PC)

    def c_e4(b):
        return rc(I_E4 + b, FP.at[b, pl.ds(2 * (1 - c), 2)], FPR.at[b, 0], PC)

    def feed_back(b):
        for r in range(2):
            g = SCALE * grad_rows(b, r)
            sva[5:6, :] += jnp.sum(g, axis=0, keepdims=True)
            GL[r * 256 : (r + 1) * 256, :] = g.astype(BF)
            GLT[:, b * 512 + r * 256 : b * 512 + (r + 1) * 256] = g.T.astype(BF)

        def active(n, carry):
            shard, rows = tile(n)
            g = nt(GL[...], WRED[shard, rows, :])
            g = (g * GH[b, n].astype(F32)).astype(BF)
            GH[b, n] = g
            EBA[n] += jnp.sum(g.astype(F32), axis=0, keepdims=True)
            return carry

        lax.fori_loop(0, 6, active, 0)

        def second(m, carry):
            rows = pl.ds(pl.multiple_of(m * 256, 256), 256)
            acc = None
            for n in range(6):
                part = nt(GH[b, n], WEXP[n // 3, rows, (n % 3) * 256 : (n % 3 + 1) * 256])
                acc = part if acc is None else acc + part
            SEC[b, :, rows] = acc.astype(BF)
            return carry

        lax.fori_loop(0, 3, second, 0)
        c_e3(b).start()

        def feed(m, carry):
            cols = pl.ds(pl.multiple_of(m * 256, 256), 256)
            acc = None
            for n in range(6):
                part = nn(ACT[b, n], WRED[n // 3, (n % 3) * 256 : (n % 3 + 1) * 256, cols])
                acc = part if acc is None else acc + part
            FP[b, :, :, cols] = acc.astype(BF).reshape(4, 128, 256)
            return carry

        lax.fori_loop(0, 3, feed, 0)
        c_e4(b).start()

    def out_rows(b, yy, cc):
        if b == 0:
            return block_out.at[pl.ds(4 + 2 * cc, 2), yy]
        return block_out.at[pl.ds(8 * yy + 2 * (b - 1) + cc, 1)]

    def bo_src(b):
        return FPR.at[0, 0] if b == 0 else FPR.at[b]

    def c_e5(b):
        return rc(I_E5 + b, bo_src(b), out_rows(b, y, c), PY)

    def c_e6(b):
        return rc(I_E6 + b, bo_src(b), out_rows(b, y, c), PC)

    def c_ef(b):
        return rc(I_EF + b, out_rows(b, 1 - y, c), out_rows(b, 1 - y, c), PC)

    def l_bo(b):
        return lc(12 + b, bo_src(b), out_rows(b, y, c))

    def finish_out(b):
        c_e4(b).wait_recv()
        two = pl.ds(2 * c, 2)
        v = MID[b, two] + SCALE * (FP[b, two].astype(F32) + FPR[b, 0].astype(F32) + rbias)
        FPR[b, 0] = v.astype(BF)
        c_e5(b).start()
        c_e6(b).start()
        l_bo(b).start()

    c_e7 = rc(I_E7, GAS0.at[1], do_out.at[0, :, y], PY)

    def l_ga(b):
        if b == 0:
            return [lc(15, GAS0.at[0], do_out.at[0, :, y])]
        two = pl.ds(2 * (b - 1), 2)
        return [lc(15 + b, GAS1.at[b - 1, 0], do_out.at[1, two]), lc(17 + b, GAS1.at[b - 1, 1], do_out.at[2, two])]

    def l_gm(b):
        return lc(20 + b, MID.at[b], gm_out.at[b])

    def middle_back(b):
        c_e3(b).wait_recv()
        for r in range(2):
            rows = slice(r * 256, (r + 1) * 256)
            g = SEC[b, rows, :].astype(F32) + GSR[b, rows, :].astype(F32)
            n, rstd = stats(MID[b, 2 * r : 2 * r + 2].reshape(256, D))
            sva[3:4, :] += jnp.sum(g * n, axis=0, keepdims=True)
            sva[4:5, :] += jnp.sum(g, axis=0, keepdims=True)
            gm = grad_rows(b, r) + norm_back(g, n, rstd, gain2)
            MID[b, 2 * r : 2 * r + 2] = gm.reshape(2, 128, D)
            low = SCALE * gm
            sva[2:3, :] += jnp.sum(low, axis=0, keepdims=True)
            GL[rows, :] = low.astype(BF)
            GL1T[:, b * 512 + r * 256 : b * 512 + (r + 1) * 256] = low.T.astype(BF)
        l_gm(b).start()
        for p in range(2):
            ga = nt(GL[...], WO[p]).astype(BF)
            if b == 0:
                GAS0[p] = ga.reshape(4, 128, W3)
            else:
                GAS1[b - 1, p] = ga.reshape(2, 2, 128, W3)
        if b == 0:
            c_e7.start()
        for k in l_ga(b):
            k.start()

    feed_back(0)
    feed_back(1)
    finish_out(0)
    middle_back(0)
    feed_back(2)
    finish_out(1)
    middle_back(1)

    def l_ab(n, kind):
        return lc(24 + n, ABS.at[n], ab_out.at[n % 3, kind, n // 3])

    def weight_grads(kind, left, right):
        def one(n, carry):
            if kind == 1:
                l_ab(n, 0).wait()
            for m in range(2):
                acc = None
                for b in range(3):
                    part = nn(
                        left[m * 384 : (m + 1) * 384, b * 512 : (b + 1) * 512], right[b, n]
                    )
                    acc = part if acc is None else acc + part
                ABS[n, 4 * m : 4 * m + 4] = acc.astype(BF).reshape(4, 96, 256)
            l_ab(n, kind).start()
            return carry

        lax.fori_loop(0, 6, one, 0)

    weight_grads(0, SECT, GH)
    finish_out(2)
    middle_back(2)
    for b in range(2):
        c_e5(b).wait_recv()
        c_ef(b).start()
    weight_grads(1, GLT, ACT)
    for p in range(2):
        for m in range(2):
            acc = None
            for b in range(3):
                part = nn(
                    GL1T[m * 384 : (m + 1) * 384, b * 512 : (b + 1) * 512],
                    AF[p, b].reshape(512, W3),
                )
                acc = part if acc is None else acc + part
            cg_out[p, 4 * m : 4 * m + 4] = acc.astype(BF).reshape(4, 96, W3)
    for n in range(6):
        at = pl.ds(8 + (t if n < 3 else 2 * (1 - y) + c), 1)
        sva[at, (n % 3) * 256 : (n % 3 + 1) * 256] = EBA[n]

    c_e5(2).wait_recv()
    c_ef(2).start()

    for m in (m_in, m_wo, m_exp, m_red):
        m.close()
    for k in (c_sv, c_wo1, c_wo2, c_e1, c_e7):
        k.wait_send()
    c_e7.wait_recv()
    for b in range(3):
        for k in (c_e2(b), c_e3(b), c_e4(b), c_e5(b)):
            k.wait_send()
        c_e6(b).wait()
        c_ef(b).wait()
        l_bo(b).wait()
        l_gm(b).wait()
        for k in l_ga(b):
            k.wait()
    winr.wait()
    for k in save_att:
        k.wait()
    for u in range(1, 3):
        for k in save_unit(u):
            k.wait()
    for n in range(6):
        l_ab(n, 1).wait()


def call_one(*args):
    any_ = pl.BlockSpec(memory_space=pl.ANY)
    vm = pl.BlockSpec(memory_space=pltpu.VMEM)
    sm = pl.BlockSpec(memory_space=pltpu.SMEM)
    S = jax.ShapeDtypeStruct
    outs = [
        (S((12, 2, 128, D), BF), any_),
        (S((3, 3, 4, 256, W3), BF), any_),
        (S((3, 8, 1024), F32), vm),
        (S((3, 2, 2, 2, 128, W3), BF), any_),
        (S((3, 4, 2, 128, W3), BF), any_),
        (S((3, 4, 128, D), F32), any_),
        (S((3 * W3, D), BF), any_),
        (S((3, 2, 2, 8, 96, 256), BF), any_),
        (S((2, 8, 96, W3), BF), vm),
        (S((16, D), F32), vm),
    ]
    V = pltpu.VMEM
    scratch = [
        V((2, 4, 2, 128, D), BF),
        V((4, 128, D), BF),
        V((4, 2, 128, D), BF),
        V((2, 3 * W3, D), BF),
        V((4, W3, D), BF),
        V((2, D, D), BF),
        V((2, D, D), BF),
        V((2, 8, D), F32),
        V((4, 256, D), BF),
        V((2, 4, 256, W3), BF),
        V((2, 4, 256, W3), BF),
        V((2, 4, 256, W3), BF),
        V((W3, 1024), BF),
        V((4, 4, 2, 2, 128, W3), BF),
        V((3, 4, 128, D), F32),
        V((3, 512, D), BF),
        V((D, 1536), BF),
        V((512, D), BF),
        V((D, 1536), BF),
        V((D, 1536), BF),
        V((3, 6, 512, 256), BF),
        V((3, 6, 512, 256), BF),
        V((3, 512, D), BF),
        V((3, 4, 128, D), BF),
        V((3, 1, 2, 128, D), BF),
        V((2, 4, 128, W3), BF),
        V((2, 2, 2, 2, 128, W3), BF),
        V((6, 1, 256), F32),
        V((6, 8, 96, 256), BF),
        pltpu.SemaphoreType.DMA((43,)),
        pltpu.SemaphoreType.DMA((43,)),
        pltpu.SemaphoreType.DMA((37,)),
    ]
    return pl.pallas_call(
        kernel_one,
        out_shape=[o for o, _ in outs],
        in_specs=[sm] + [any_] * 6 + [vm] * 8,
        out_specs=[s for _, s in outs],
        scratch_shapes=scratch,
        compiler_params=pltpu.CompilerParams(
            collective_id=0, has_side_effects=True, vmem_limit_bytes=VMEM_LIMIT
        ),
    )(*args)


ORDERS = ("y0z", "0zy", "102y", "102y", "y0z", "0zy", "z0y")
COLS = (256, 256, 256, W3, 256, 256, 64)


def ways(axis):
    return 4 if axis == "z" else 2


def set_shapes(index):
    lead = (2,) if index < 3 else ()
    tail = (96, COLS[index])
    axes = ["y", "2", "1", "0"]
    shapes = [lead + (2,) * 4 + tail]
    places = []
    for axis in ORDERS[index]:
        at = axes.index("2" if axis == "z" else axis)
        del axes[at : at + ways(axis) // 2]
        places.append(len(lead) + at)
        shapes.append(lead + (2,) * len(axes) + tail)
    return shapes, places


def sum_phases(n_dp):
    bits = [1 << k for k in range(n_dp.bit_length() - 1)]
    rest = bits[1:]
    return [("c",), ("y", bits[0])] + [tuple(rest[k : k + 2]) for k in range(0, len(rest), 2)]


def kernel_two(
    n_dp, len_ref, tok, qkv, lse, att, do, gm, win, winr, ab, cg, sva, g1, s1,
    tok_grad, a_out, b_out, c_out, d_out, vec_out, eb_out, qv_out,
    TOK, QS, KS, VS, AT, DO, GM, WIN, NRMT, KT, DEL, DQT, DP, QVB, GN, GNR, GNS, GNSR, SHS, SHR, TG, TGS,
    ACCW, DW0, DW1, DW2, SVR, SVC, *rest,
):
    ssem, rsem, lsem = rest[-3:]
    bufs = rest[:-3]
    dp = lax.axis_index("dp")
    t = lax.axis_index("tensor")
    y = t // 2
    c = t % 2
    PY = (dp, 2 * (1 - y) + c)
    PC = (dp, 2 * y + 1 - c)
    low = n_dp // 4
    mine = {"y": 0, "z": dp // low}
    stride = {"2": n_dp // 2, "1": n_dp // 4, "0": n_dp // 8}
    for a, v in stride.items():
        mine[a] = (dp // v) % 2

    def peer(axis, r):
        if axis == "y":
            return PY
        if axis == "z":
            return (((mine["z"] + r) % 4) * low + dp % low, t)
        return (flip(dp, stride[axis]), t)

    phases = sum_phases(n_dp)

    def sum_peer(k, mask):
        at_dp, at_t = dp, t
        for j, bit in enumerate(phases[k]):
            if (mask >> j) & 1:
                if bit == "c":
                    at_t = flip(at_t, 1)
                elif bit == "y":
                    at_t = flip(at_t, 2)
                else:
                    at_dp = flip(at_dp, bit)
        return (at_dp, at_t)

    def sum_bit(k, j):
        bit = phases[k][j]
        return c if bit == "c" else y if bit == "y" else (dp // bit) % 2

    def rc(i, src, dst, dev):
        return remote(src, dst, ssem.at[i], rsem.at[i], dev)

    def lc(i, src, dst):
        return pltpu.make_async_copy(src, dst, lsem.at[i])

    sets = []
    pos = 0
    for index in range(7):
        shapes, places = set_shapes(index)
        whole = ab.at[index] if index < 3 else (cg, DW0, DW1, DW2)[index - 3]
        steps = len(ORDERS[index])
        sums = [whole] + list(bufs[pos : pos + steps - 1])
        recvs = bufs[pos + steps - 1 : pos + 2 * steps - 1]
        pos += 2 * steps - 1
        sets.append((shapes, places, sums, recvs))

    def one_of(axis, k):
        return (k // 2, k % 2) if axis == "z" else (k,)

    def pick(ref, place, axis, k):
        return ref.at[(slice(None),) * place + one_of(axis, k)]

    def set_copies(index, step):
        shapes, places, sums, recvs = sets[index]
        order = ORDERS[index]
        axis = order[step]
        base = 5 * index + sum(ways(a) - 1 for a in order[:step])
        return [
            rc(
                base + r - 1,
                pick(sums[step], places[step], axis, (mine[axis] + r) % ways(axis)),
                recvs[step].at[r - 1],
                peer(axis, r),
            )
            for r in range(1, ways(axis))
        ]

    def set_begin(index, step):
        for k in set_copies(index, step):
            k.start()

    def keep_load(index):
        shapes, places, sums, recvs = sets[index]
        axis = ORDERS[index][0]
        return lc(20 + index, pick(sums[0], places[0], axis, mine[axis]), sums[1])

    def set_step(index, step):
        shapes, places, sums, recvs = sets[index]
        axis = ORDERS[index][step]
        for k in set_copies(index, step):
            k.wait_recv()
        in_place = index < 3 and step == 0
        if in_place:
            keep_load(index).wait()
        lead = shapes[step + 1][:-2]
        for flat in range(math.prod(lead)):
            where = []
            left = flat
            for size in reversed(lead):
                where.append(left % size)
                left //= size
            where = tuple(reversed(where))
            if in_place:
                v = sums[1][where]
            else:
                place = places[step]
                v = sums[step][where[:place] + one_of(axis, mine[axis]) + where[place:]]
            v = v.astype(F32)
            for r in range(ways(axis) - 1):
                v = v + recvs[step][(r,) + where].astype(F32)
            if step + 1 < len(ORDERS[index]):
                sums[step + 1][where] = v.astype(BF)
            elif index < 3:
                out = (a_out, b_out)[where[0]]
                out[:, index * 256 : (index + 1) * 256] = v
            elif index == 3:
                c_out[...] = v
            else:
                start = (index - 4) * 256
                d_out[:, start : start + COLS[index]] = v
        if step + 1 < len(ORDERS[index]):
            set_begin(index, step + 1)

    lds = [
        lc(0, tok.at[pl.ds(4, 4)], TOK.at[0]),
        lc(1, tok.at[pl.ds(8 * y, 4)], TOK.at[1]),
        lc(2, qkv.at[:, 0], QS),
        lc(3, qkv.at[:, 1], KS),
        lc(4, qkv.at[:, 2], VS),
        lc(5, att, AT),
        lc(6, do, DO),
        lc(7, win, WIN.at[0]),
        lc(8, winr, WIN.at[1]),
        lc(9, gm.at[0, c], GM.at[0]),
        lc(15, gm.at[pl.ds(1, 2), :, c], GM.at[pl.ds(1, 2)]),
    ]
    for k in lds:
        k.start()
    others = [(k, mask) for k in range(len(phases)) for mask in range(1, 1 << len(phases[k]))]
    greet(
        [PY, PC, peer("0", 1), peer("1", 1), peer("2", 1)]
        + [peer("z", r) for r in range(1, 4)]
        + [sum_peer(k, mask) for k, mask in others if (k, mask) not in ((0, 1), (1, 1))]
    )
    for index in range(4):
        set_begin(index, 0)
        if index < 3:
            keep_load(index).start()
    gain1 = row(g1)
    shift1 = row(s1)
    SVC[...] = sva[...]
    QVB[...] = jnp.zeros_like(QVB)
    DQT[...] = jnp.zeros_like(DQT)
    for k in lds:
        k.wait()

    def normed(k, carry):
        n, _ = stats(TOK[k // 4, k % 4].reshape(256, D).astype(F32))
        cols = pl.ds(pl.multiple_of((k % 4) * 256, 256), 256)
        NRMT[k // 4, :, cols] = (n * gain1 + shift1).T.astype(BF)
        return carry

    lax.fori_loop(0, 8, normed, 0)

    def prepare(u, carry):
        for i in range(4):
            cols = slice(i * 256, (i + 1) * 256)
            KT[u, :, cols] = KS[u, i].astype(F32).T.astype(BF)
            od = AT[u, i // 2, i % 2].reshape(256, W3).astype(F32) * DO[u, i].reshape(256, W3).astype(F32)
            DEL[u, 0:3, cols] = jnp.sum(od.T.reshape(3, HD, 256), axis=1)
        return carry

    lax.fori_loop(0, 3, prepare, 0)

    row_k = lax.broadcasted_iota(jnp.int32, (256, 256), 0)
    col_q = lax.broadcasted_iota(jnp.int32, (256, 256), 1)

    def block(u, j):
        w = u // 2
        nz = (u + 1) // 2
        length = len_ref[(1 - nz) + nz * 2 * y]
        inside = (row_k + j * 256) < length
        tiles_k, tiles_v = [], []
        for h in range(3):
            lanes = slice(h * HD, (h + 1) * HD)
            kt = head_tile(KS[u, j], h)
            vt = head_tile(VS[u, j], h)
            dk = dv = None
            for i in range(j, 4):
                cols = slice(i * 256, (i + 1) * 256)
                qh = head_tile(QS[u, i], h)
                gh = head_tile(DO[u, i].reshape(256, W3), h)
                if h < 2:
                    qh, gh = head_lanes(qh, h), head_lanes(gh, h)
                p = jnp.exp(nt(kt, qh) - lse[u, h : h + 1, cols])
                ok = inside & (row_k <= col_q) if i == j else inside
                p = jnp.where(ok, p, 0.0)
                ds = (p * (nt(vt, gh) - DEL[u, h : h + 1, cols])).astype(BF)
                pb = p.astype(BF)
                a, b = nn(pb, gh), nn(ds, qh)
                dv = a if dv is None else dv + a
                dk = b if dk is None else dk + b
                DQT[u, lanes, cols] += nn(KT[u, lanes, j * 256 : (j + 1) * 256], ds)
            tiles_k.append(dk)
            tiles_v.append(dv)
        gk = jnp.concatenate([tiles_k[0] + tiles_k[1], tiles_k[2]], axis=1)
        gv = jnp.concatenate([tiles_v[0] + tiles_v[1], tiles_v[2]], axis=1)
        gq = DQT[u, :, j * 256 : (j + 1) * 256].T * 0.125
        gq, gk, gv = gq.astype(BF), gk.astype(BF), gv.astype(BF)
        DP[u, j] = jnp.concatenate([gq, gk, gv], axis=1)
        QVB[w, 0:1, 0:W3] += jnp.sum(gq.astype(F32), axis=0, keepdims=True)
        QVB[w, 0:1, 256 : 256 + W3] += jnp.sum(gv.astype(F32), axis=0, keepdims=True)

    def finish_rows(g, x, middle):
        n, rstd = stats(x.astype(F32))
        SVC[0:1, :] += jnp.sum(g * n, axis=0, keepdims=True)
        SVC[1:2, :] += jnp.sum(g, axis=0, keepdims=True)
        return (middle + norm_back(g, n, rstd, gain1)).astype(BF)

    for j in range(4):
        block(0, j)
    for i in range(4):
        acc = nn(DP[0, i], WIN[0])
        GNS[i] = acc.astype(BF).reshape(2, 128, D)
    c_core = rc(39, GNS.at[pl.ds(2 * (1 - c), 2)], GNSR, PC)
    c_core.start()
    c_y = rc(40, SHS, SHR, PY)

    def share_rows():
        c_core.wait_recv()
        for k in range(2):
            v = GNS[2 * c + k, 1 - y].astype(F32) + GNSR[k, 1 - y].astype(F32)
            SHS[k] = v.astype(BF)
        c_y.start()

    def shared_out(yy, cc):
        return tok_grad.at[pl.ds(4 + 2 * cc, 2), yy]

    t_y = rc(53, TGS, shared_out(y, c), PY)
    t_c = rc(54, TGS, shared_out(y, c), PC)
    t_f = rc(55, shared_out(1 - y, c), shared_out(1 - y, c), PC)
    t_l = lc(10, TGS, shared_out(y, c))

    def finish_shared():
        c_y.wait_recv()
        for k in range(2):
            g = GNS[2 * c + k, y].astype(F32) + GNSR[k, y].astype(F32) + SHR[k].astype(F32)
            TGS[k] = finish_rows(g, TOK[0, 2 * c + k, y], GM[0, k])
        t_y.start()
        t_c.start()
        t_l.start()

    def c_gn(j):
        return rc(35 + j, GN.at[j, 1 - c], GNR.at[j], PC)

    def own_out(j, yy, cc):
        return tok_grad.at[8 * yy + j, cc]

    def c_own(j, k):
        if k == 0:
            return rc(41 + j, TG.at[j], own_out(j, y, c), PY)
        if k == 1:
            return rc(45 + j, TG.at[j], own_out(j, y, c), PC)
        if k == 2:
            return rc(49 + j, own_out(j, 1 - y, c), own_out(j, 1 - y, c), PC)
        return lc(11 + j, TG.at[j], own_out(j, y, c))

    def rows_back(j):
        acc = nn(DP[1, j], WIN[0]) + nn(DP[2, j], WIN[1])
        GN[j] = acc.astype(BF).reshape(2, 128, D)
        c_gn(j).start()

    def finish_own(j):
        c_gn(j).wait_recv()
        g = GN[j, c].astype(F32) + GNR[j].astype(F32)
        TG[j] = finish_rows(g, TOK[1, j, c], GM[1 + j // 2, j % 2])
        for k in (0, 1, 3):
            c_own(j, k).start()

    def pass_own(j):
        c_own(j, 0).wait_recv()
        c_own(j, 2).start()

    def own_blocks(j):
        def one(u, carry):
            block(u, j)
            return carry

        lax.fori_loop(1, 3, one, 0)

    def input_grads(first):
        for w in range(2):
            for m in range(2):
                rows = slice(m * 384, (m + 1) * 384)
                if first:
                    acc = nn(NRMT[1, rows, 0:768], DP[1 + w, 0:3].reshape(768, 3 * W3))
                    if w == 0:
                        acc = acc + nn(NRMT[0, rows, :], DP[0].reshape(1024, 3 * W3))
                    ACCW[w, rows, :] = acc
                else:
                    acc = ACCW[w, rows, :] + nn(NRMT[1, rows, 768:1024], DP[1 + w, 3])
                    for k, ref in enumerate((DW0, DW1, DW2)):
                        cols = acc[:, 256 * k : min(256 * (k + 1), 3 * W3)]
                        ref[w, m] = cols.astype(BF).reshape(2, 2, 96, -1)

    def sum_copy(k, mask):
        return rc(
            56 + others.index((k, mask)), SVR.at[k, 0], SVR.at[k, mask], sum_peer(k, mask)
        )

    def sum_begin(k):
        for mask in range(1, 1 << len(phases[k])):
            sum_copy(k, mask).start()

    def sum_step(k):
        count = len(phases[k])
        for mask in range(1, 1 << count):
            sum_copy(k, mask).wait_recv()
        total = None
        for a in range(1 << count):
            slot = sum((((a >> j) + sum_bit(k, j)) % 2) * (1 << j) for j in range(count))
            total = SVR[k, slot] if total is None else total + SVR[k, slot]
        if k + 1 < len(phases):
            SVR[k + 1, 0] = total
            sum_begin(k + 1)
        else:
            SVC[...] = total

    own_blocks(0)
    share_rows()
    rows_back(0)
    for index in range(4):
        set_step(index, 0)
    own_blocks(1)
    finish_own(0)
    rows_back(1)
    finish_shared()
    own_blocks(2)
    pass_own(0)
    finish_own(1)
    rows_back(2)
    for index in range(4):
        set_step(index, 1)
    input_grads(True)
    finish_own(2)
    t_y.wait_recv()
    t_f.start()
    own_blocks(3)
    rows_back(3)
    input_grads(False)
    for index in range(4, 7):
        set_begin(index, 0)
    pass_own(1)
    finish_own(3)
    for w in range(2):
        SVC[pl.ds(12 + (t if w == 0 else 2 * (1 - y) + c), 1), :] = QVB[w]
    SVR[0, 0] = SVC[...]
    sum_begin(0)
    for index in range(4):
        set_step(index, 2)
    pass_own(2)
    sum_step(0)
    for index in range(4, 7):
        set_step(index, 0)
    pass_own(3)
    sum_step(1)
    for index in range(4, 7):
        set_step(index, 1)
    for index in range(2, 4):
        set_step(index, 3)
    for k in range(2, len(phases)):
        sum_step(k)
    for index in range(4, 7):
        set_step(index, 2)
    both = lax.broadcasted_iota(jnp.int32, (8, 1), 0) >= 2
    vec_out[...] = jnp.where(both, 0.5, 1.0) * SVC[0:8, :]
    eb_out[...] = SVC[pl.ds(8 + t, 1), :]
    qv_out[...] = SVC[pl.ds(12 + t, 1), :]

    for index in range(7):
        for step in range(len(ORDERS[index])):
            for k in set_copies(index, step):
                k.wait_send()
    for k, mask in others:
        sum_copy(k, mask).wait_send()
    for j in range(4):
        c_gn(j).wait_send()
        c_own(j, 0).wait_send()
        for k in (1, 2, 3):
            c_own(j, k).wait()
    c_core.wait_send()
    c_y.wait_send()
    t_y.wait_send()
    t_c.wait()
    t_f.wait()
    t_l.wait()


def call_two(n_dp, *args):
    any_ = pl.BlockSpec(memory_space=pl.ANY)
    vm = pl.BlockSpec(memory_space=pltpu.VMEM)
    sm = pl.BlockSpec(memory_space=pltpu.SMEM)
    S = jax.ShapeDtypeStruct
    outs = [
        (S((12, 2, 128, D), BF), any_),
        (S((96, D), F32), vm),
        (S((96, D), F32), vm),
        (S((96, W3), F32), vm),
        (S((96, 3 * W3), F32), vm),
        (S((8, D), F32), vm),
        (S((1, D), F32), vm),
        (S((1, D), F32), vm),
    ]
    V = pltpu.VMEM
    phases = sum_phases(n_dp)
    sums = sum((1 << len(v)) - 1 for v in phases)
    scratch = [
        V((2, 4, 2, 128, D), BF),
        V((3, 4, 256, W3), BF),
        V((3, 4, 256, W3), BF),
        V((3, 4, 256, W3), BF),
        V((3, 2, 2, 2, 128, W3), BF),
        V((3, 4, 2, 128, W3), BF),
        V((3, 2, 128, D), F32),
        V((2, 3 * W3, D), BF),
        V((2, D, 1024), BF),
        V((3, W3, 1024), BF),
        V((3, 8, 1024), F32),
        V((3, W3, 1024), F32),
        V((3, 4, 256, 3 * W3), BF),
        V((2, 1, D), F32),
        V((4, 2, 128, D), BF),
        V((4, 128, D), BF),
        V((4, 2, 128, D), BF),
        V((2, 2, 128, D), BF),
        V((2, 128, D), BF),
        V((2, 128, D), BF),
        V((4, 128, D), BF),
        V((2, 128, D), BF),
        V((2, D, 3 * W3), F32),
        V((2, 2, 2, 2, 96, 256), BF),
        V((2, 2, 2, 2, 96, 256), BF),
        V((2, 2, 2, 2, 96, 64), BF),
        V((len(phases), 4, 16, D), F32),
        V((16, D), F32),
    ]
    for index in range(7):
        shapes, _ = set_shapes(index)
        scratch += [V(shape, BF) for shape in shapes[1:-1]]
        scratch += [V((ways(a) - 1,) + shapes[k + 1], BF) for k, a in enumerate(ORDERS[index])]
    scratch += [
        pltpu.SemaphoreType.DMA((56 + sums,)),
        pltpu.SemaphoreType.DMA((56 + sums,)),
        pltpu.SemaphoreType.DMA((23,)),
    ]
    return pl.pallas_call(
        functools.partial(kernel_two, n_dp),
        out_shape=[o for o, _ in outs],
        in_specs=[sm, any_, any_, vm] + [any_] * 6 + [vm] * 4,
        out_specs=[s for _, s in outs],
        scratch_shapes=scratch,
        compiler_params=pltpu.CompilerParams(
            collective_id=1, has_side_effects=True, vmem_limit_bytes=VMEM_LIMIT
        ),
    )(*args)


def kernel_three(
    block_in, tok_in, a_in, b_in, c_in, d_in, rep, eb, qv,
    block_out, tok_out, a_out, b_out, c_out, d_out, v0, v1, v2, v3, v4, v5, e_out, q_out,
):
    block_out[...] = block_in[...]
    tok_out[...] = tok_in[...]

    @pl.when(pl.program_id(0) == 0)
    def _():
        a_out[...] = a_in[...]
        b_out[...] = b_in[...]
        c_out[...] = c_in[...].T
        for j in range(3):
            d_out[j] = d_in[:, j * W3 : (j + 1) * W3]
        for k, ref in enumerate((v0, v1, v2, v3, v4, v5)):
            ref[...] = rep[k : k + 1, :].reshape(D)
        e_out[...] = eb[...].reshape(D)
        q_out[0:1, :] = qv[:, 0:W3]
        q_out[1:2, :] = qv[:, 256 : 256 + W3]


def call_three(*args):
    part = pl.BlockSpec((3, 2, 128, D), lambda i: (i, 0, 0, 0))
    vm = pl.BlockSpec(memory_space=pltpu.VMEM)
    S = jax.ShapeDtypeStruct
    outs = [S((12, 2, 128, D), BF)] * 2 + [S((96, D), F32)] * 2
    outs += [S((W3, 96), F32), S((3, 96, W3), F32)] + [S((D,), F32)] * 7 + [S((2, W3), F32)]
    return pl.pallas_call(
        kernel_three,
        out_shape=outs,
        grid=(4,),
        in_specs=[part] * 2 + [vm] * 7,
        out_specs=[part] * 2 + [vm] * 12,
        compiler_params=pltpu.CompilerParams(vmem_limit_bytes=VMEM_LIMIT),
    )(*args)


def body(
    n_dp, tokens, lengths, first_gain, first_shift, input_weight, query_value_bias, output_weight,
    output_bias, second_gain, second_shift, expand_weight, expand_bias, reduce_weight, reduce_bias,
    cotangent,
):
    tok = tokens.reshape(12, 2, 128, D)
    cot = cotangent.reshape(12, 2, 128, D)
    win = jnp.transpose(input_weight, (1, 2, 0)).reshape(3 * W3, D)
    block_out, qkv, lse, att, do, gm, winr, ab, cg, sva = call_one(
        lengths, tok, cot, win, output_weight, expand_weight, reduce_weight, first_gain, first_shift,
        output_bias, second_gain, second_shift, reduce_bias, expand_bias, query_value_bias,
    )
    found = call_two(
        n_dp, lengths, tok, qkv, lse, att, do, gm.reshape(3, 2, 2, 128, D), win, winr,
        ab.reshape(3, 2, 2, 2, 2, 2, 96, 256), cg.reshape(2, 2, 2, 2, 96, W3), sva, first_gain, first_shift,
    )
    block_out, tok_grad, a, b, cc, d, v0, v1, v2, v3, v4, v5, eb, qv = call_three(block_out, *found)
    left = n_dp // 8
    if left > 1:
        groups = [list(range(k * left, (k + 1) * left)) for k in range(8)]
        a, b, cc, d = [
            lax.psum_scatter(v, "dp", scatter_dimension=at, axis_index_groups=groups, tiled=True)
            for v, at in ((a, 0), (b, 0), (cc, 1), (d, 1))
        ]
    return (
        block_out.reshape(tokens.shape),
        tok_grad.reshape(tokens.shape),
        v0,
        v1,
        jnp.transpose(d, (1, 0, 2)),
        qv,
        cc,
        v2,
        v3,
        v4,
        a,
        eb,
        b.T,
        v5,
    )


def solution(mesh):
    return jax.shard_map(
        functools.partial(body, mesh.shape["dp"]),
        mesh=mesh,
        in_specs=(
            P("dp", None),
            P("dp"),
            P(),
            P(),
            P(None, None, "tensor"),
            P(None, "tensor"),
            P("tensor", None),
            P(),
            P(),
            P(),
            P(None, "tensor"),
            P("tensor"),
            P("tensor", None),
            P(),
            P("dp", None),
        ),
        out_specs=(
            P("dp", None),
            P("dp", None),
            P(),
            P(),
            P("dp", None, "tensor"),
            P(None, "tensor"),
            P("tensor", "dp"),
            P(),
            P(),
            P(),
            P("dp", "tensor"),
            P("tensor"),
            P("tensor", "dp"),
            P(),
        ),
        check_vma=False,
    )
```

```python
import functools
import math

import jax
import jax.numpy as jnp
from jax import lax
from jax.experimental import pallas as pl
from jax.experimental.pallas import tpu as pltpu
from jax.sharding import PartitionSpec as P

MESH = pl.DeviceIdType.MESH
F32 = jnp.float32
BF = jnp.bfloat16
D = 768
W3 = 192
HD = 64
EPS = 1e-05
MASKED = -1e30
SCALE = 1.0 / math.sqrt(24.0)
VMEM_LIMIT = 65280 * 1024


def nn(a, b):
    return lax.dot_general(a, b, (((1,), (0,)), ((), ())), preferred_element_type=F32)


def nt(a, b):
    return lax.dot_general(a, b, (((1,), (1,)), ((), ())), preferred_element_type=F32)


def remote(src, dst, ssem, rsem, dev):
    return pltpu.make_async_remote_copy(
        src_ref=src, dst_ref=dst, send_sem=ssem, recv_sem=rsem, device_id=dev, device_id_type=MESH
    )


def flip(i, stride):
    return i + stride * (1 - 2 * ((i // stride) % 2))


def greet(peers):
    barrier = pltpu.get_barrier_semaphore()
    for peer in peers:
        pl.semaphore_signal(barrier, inc=1, device_id=peer, device_id_type=MESH)
    pl.semaphore_wait(barrier, len(peers))


def stats(v):
    mean = jnp.mean(v, axis=-1, keepdims=True)
    centre = v - mean
    rstd = lax.rsqrt(jnp.mean(centre * centre, axis=-1, keepdims=True) + EPS)
    return centre * rstd, rstd


def norm_back(grad, n, rstd, gain):
    e = grad * gain
    return rstd * (
        e - jnp.mean(e, axis=-1, keepdims=True) - n * jnp.mean(e * n, axis=-1, keepdims=True)
    )


def row(ref):
    return ref[...].astype(F32).reshape(1, D)


def head_lanes(tile, h):
    lane = lax.broadcasted_iota(jnp.int32, tile.shape, 1)
    keep = (lane < HD) if h % 2 == 0 else (lane >= HD)
    return jnp.where(keep, tile, jnp.zeros_like(tile))


def head_tile(x, h):
    return x[:, :128] if h < 2 else x[:, 128:192]


def gelu_both(v):
    c = math.sqrt(2.0 / math.pi)
    sq = v * v
    t = jnp.tanh(c * v * (1.0 + 0.044715 * sq))
    half = 0.5 * (1.0 + t)
    slope = half + (0.5 * c) * v * (1.0 - t * t) * (1.0 + (3.0 * 0.044715) * sq)
    return v * half, slope


def kernel_one(
    len_ref, tok, cot, win, wo, wexp, wred, g1, s1, ob, g2, s2, rb, eb, qvb,
    block_out, qkv_out, lse_out, att_out, do_out, gm_out, winr_out, ab_out, cg_out, sva,
    TOK, COT0, COT1, WIN, WO, WEXP, WRED, SV, NRM, QS, KS, VS, VT, AF, MID, SEC, SECT, GL, GLT, GL1T,
    ACT, GH, GSR, FP, FPR, GAS0, GAS1, EBA, ABS, ssem, rsem, lsem,
):
    dp = lax.axis_index("dp")
    t = lax.axis_index("tensor")
    y = t // 2
    c = t % 2
    PY = (dp, 2 * (1 - y) + c)
    PC = (dp, 2 * y + 1 - c)
    PX = (flip(dp, 1), t)
    PZ = (flip(dp, 2), t)
    bx = dp % 2
    bz = (dp // 2) % 2

    def rc(i, src, dst, dev):
        return remote(src, dst, ssem.at[i], rsem.at[i], dev)

    def lc(i, src, dst):
        return pltpu.make_async_copy(src, dst, lsem.at[i])

    class Spread:
        def __init__(self, base, src, full, rows, first):
            self.base, self.src, self.full, self.rows, self.first = base, src, full, rows // 4, first

        def part(self, ref, quarter, start=0, size=None):
            return ref.at[pl.ds(pl.multiple_of(quarter * self.rows + start, 16), size or self.rows)]

        def copy(self, kind):
            q, qx, qz = 2 * bx + bz, 2 * (1 - bx) + bz, 2 * bx + 1 - bz
            f, s = self.first, self.rows - self.first
            i = self.base + "yxzab".index(kind)
            if kind == "y":
                return rc(i, self.part(self.src, q), self.part(self.full, q), PY)
            if kind in "xz":
                return rc(
                    i, self.part(self.full, q), self.part(self.full, q), PX if kind == "x" else PZ
                )
            if kind == "a" and f == 0:
                q = 3 - q
                return rc(i, self.part(self.src, q), self.part(self.full, q), PY)
            if kind == "a":
                return rc(i, self.part(self.full, qz, 0, f), self.part(self.full, qz, 0, f), PX)
            return rc(i, self.part(self.full, qx, f, s), self.part(self.full, qx, f, s), PZ)

        def begin(self):
            self.copy("y").start()

        def pass_on(self):
            self.copy("y").wait_recv()
            self.copy("x").start()
            self.copy("z").start()
            if self.first == 0:
                self.copy("a").start()

        def pass_again(self):
            self.copy("x").wait_recv()
            self.copy("z").wait_recv()
            self.copy("a").start()
            self.copy("b").start()

        def ready(self):
            for kind in "xza" if self.first == 0 else "ab":
                self.copy(kind).wait_recv()

        def close(self):
            for kind in "yxza" if self.first == 0 else "yxzab":
                self.copy(kind).wait_send()

    m_in = Spread(0, win, WIN.at[1], 3 * W3, 0)
    m_wo = Spread(5, wo, WO.at[1], W3, 0)
    m_exp = Spread(10, wexp, WEXP.at[1], D, 96)
    m_red = Spread(15, wred, WRED.at[1], D, 96)
    I_SV, I_WO1, I_WO2, I_E1, I_E7 = 20, 21, 22, 23, 24
    I_E2, I_E3, I_E4, I_E5, I_E6, I_EF = 25, 31, 34, 37, 40, 43

    ld_tok = [lc(0, tok.at[pl.ds(4, 4)], TOK.at[0]), lc(1, tok.at[pl.ds(8 * y, 4)], TOK.at[1])]
    ld_win = lc(2, win, WIN.at[0])
    ld_rest = [
        lc(3, wo, WO.at[0]),
        lc(4, wexp, WEXP.at[0]),
        lc(5, wred, WRED.at[0]),
        lc(6, cot.at[pl.ds(4, 4), y], COT0),
        lc(7, cot.at[pl.ds(8 * y, 4)], COT1),
    ]
    ld_tok[0].start()
    ld_win.start()
    SV[0] = jnp.zeros((8, D), F32)
    SV[0, 0:1, :] = row(eb)
    SV[0, 1:3, 0:W3] = qvb[...].astype(F32)

    greet([PY, PC, PX, PZ])
    c_sv = rc(I_SV, SV.at[0], SV.at[1], PY)
    c_sv.start()
    m_in.begin()
    m_wo.begin()
    c_wo1 = rc(I_WO1, wo, WO.at[2], PC)
    c_wo1.start()
    ld_tok[1].start()
    for k in ld_rest:
        k.start()
    sva[...] = jnp.zeros_like(sva)
    EBA[...] = jnp.zeros_like(EBA)

    gain1, shift1 = row(g1), row(s1)
    obias, gain2, shift2, rbias = row(ob), row(g2), row(s2), row(rb)

    c_e1 = rc(I_E1, AF.at[0, 3], AF.at[1, 0], PY)

    def c_e2(b, p):
        return rc(I_E2 + 2 * b + p, AF.at[p, b], AF.at[2 + p, b], PC)

    row_k = lax.broadcasted_iota(jnp.int32, (256, 256), 0)
    col_q = lax.broadcasted_iota(jnp.int32, (256, 256), 1)

    def save_unit(u):
        return [
            lc(8 + j + 26 * (u % 2), ref.at[u % 2], qkv_out.at[u, j])
            for j, ref in enumerate((QS, KS, VS))
        ]

    def unit(u, carry):
        nz = (u + 1) // 2
        w = u // 2
        length = len_ref[(1 - nz) + nz * 2 * y]

        @pl.when(u == 0)
        def _():
            ld_tok[0].wait()

        @pl.when(u == 1)
        def _():
            ld_tok[1].wait()

        @pl.when(u < 2)
        def _():
            for i in range(4):
                n, _ = stats(TOK[u, i].reshape(256, D).astype(F32))
                NRM[i] = (n * gain1 + shift1).astype(BF)

        @pl.when(u == 0)
        def _():
            ld_win.wait()

        @pl.when(u == 2)
        def _():
            for k in save_unit(0):
                k.wait()
            m_in.ready()
            c_sv.wait_recv()

        for i in range(4):
            x = NRM[i]
            q = nt(x, WIN[w, 0:W3, :]) + SV[w, 1:2, 0:W3]
            QS[u % 2, i] = q.astype(BF) * jnp.asarray(0.125, BF)
            k = nt(x, WIN[w, W3 : 2 * W3, :])
            KS[u % 2, i] = k.astype(BF)
            v = nt(x, WIN[w, 2 * W3 : 3 * W3, :]) + SV[w, 2:3, 0:W3]
            VS[u % 2, i] = v.astype(BF)
            VT[:, i * 256 : (i + 1) * 256] = v.T.astype(BF)
        for k in save_unit(u):
            k.start()

        for i in range(4):
            qi = QS[u % 2, i]
            outs = []
            for h in range(3):
                qh = head_tile(qi, h)
                if h < 2:
                    qh = head_lanes(qh, h)
                parts = []
                for kb in range(i + 1):
                    s = nt(head_tile(KS[u % 2, kb], h), qh)
                    ok = (row_k + kb * 256) < length
                    if kb == i:
                        ok = ok & (row_k <= col_q)
                    parts.append(jnp.where(ok, s, MASKED))
                top = functools.reduce(
                    jnp.maximum, [jnp.max(s, axis=0, keepdims=True) for s in parts]
                )
                total = jnp.zeros_like(top)
                acc = jnp.zeros((HD, 256), F32)
                for kb, s in enumerate(parts):
                    p = jnp.exp(s - top)
                    total = total + jnp.sum(p, axis=0, keepdims=True)
                    acc = acc + nn(
                        VT[h * HD : (h + 1) * HD, kb * 256 : (kb + 1) * 256], p.astype(BF)
                    )
                outs.append(acc * (1.0 / total))
                lse_out[u, h : h + 1, i * 256 : (i + 1) * 256] = top + jnp.log(total)
            o = jnp.concatenate(outs, axis=0).T.astype(BF)
            for hh in range(2):
                blk = (1 - nz) * (3 * ((hh + y) % 2)) + nz * (1 + i // 2)
                s0 = (1 - nz) * (i // 2) + nz * (i % 2)
                s1 = (1 - nz) * (i % 2) + nz * hh
                AF[w, blk, s0, s1] = o[hh * 128 : (hh + 1) * 128]

            if i == 1:

                @pl.when(u == 1)
                def _():
                    m_exp.begin()

                @pl.when(u == 2)
                def _():
                    c_e2(1, 1).start()

        @pl.when(u == 0)
        def _():
            m_in.pass_on()
            c_e2(0, 0).start()

        @pl.when(u == 1)
        def _():
            m_wo.pass_on()
            c_e1.start()
            m_red.begin()
            c_e2(1, 0).start()
            c_e2(2, 0).start()

        @pl.when(u == 2)
        def _():
            c_e2(2, 1).start()

        return carry

    lax.fori_loop(0, 3, unit, 0)
    save_att = [
        lc(30, AF.at[0, 0], att_out.at[0, :, :, y]),
        lc(31, AF.at[0, 3], att_out.at[0, :, :, 1 - y]),
        lc(32, AF.at[0, pl.ds(1, 2)], att_out.at[1]),
        lc(33, AF.at[1, pl.ds(1, 2)], att_out.at[2]),
    ]
    for k in save_att:
        k.start()
    m_exp.pass_on()
    m_wo.ready()
    c_wo2 = rc(I_WO2, WO.at[1], WO.at[3], PC)
    c_wo2.start()
    winr = lc(11, WIN.at[1], winr_out)
    winr.start()
    for k in ld_rest:
        k.wait()
    c_wo1.wait_recv()
    c_wo2.wait_recv()

    def tok_rows(b, r):
        if b == 0:
            v = jnp.concatenate([TOK[0, 2 * r, y], TOK[0, 2 * r + 1, y]], axis=0)
        else:
            v = TOK[1, 2 * (b - 1) + r].reshape(256, D)
        return v.astype(F32)

    for b in (1, 2, 0):
        for p in range(2):
            c_e2(b, p).wait_recv()
        for r in range(2):
            acc = None
            for p in range(4):
                part = nn(AF[p, b, r].reshape(256, W3), WO[p])
                acc = part if acc is None else acc + part
            mid = tok_rows(b, r) + SCALE * (acc + obias)
            MID[b, 2 * r : 2 * r + 2] = mid.reshape(2, 128, D)
            n, _ = stats(mid)
            sec = n * gain2 + shift2
            SEC[b, r * 256 : (r + 1) * 256, :] = sec.astype(BF)
            SECT[:, b * 512 + r * 256 : b * 512 + (r + 1) * 256] = sec.T.astype(BF)
        if b == 1:
            c_e1.wait_recv()
            c_e2(0, 1).start()
        if b == 2:
            m_red.pass_on()
    m_exp.pass_again()

    def tile(n):
        return n // 3, pl.ds(pl.multiple_of((n % 3) * 256, 256), 256)

    def hidden_part(b, first):
        def hidden(n, carry):
            shard, cols = tile(n)
            h = nn(SEC[b], WEXP[shard, :, cols]) + SV[shard, 0:1, cols]
            act, slope = gelu_both(h)
            ACT[b, n] = act.astype(BF)
            GH[b, n] = slope.astype(BF)
            return carry

        lax.fori_loop(first, first + 3, hidden, 0)

    ridx = lax.broadcasted_iota(jnp.int32, (256, 1), 0)

    def grad_rows(b, r):
        if b == 0:
            g = COT0[2 * r : 2 * r + 2].reshape(256, D).astype(F32)
            p = 512 * r + 256 * (ridx // 128) + 128 * y + ridx % 128
            length = len_ref[1]
        else:
            g = COT1[2 * (b - 1) + r].reshape(256, D).astype(F32)
            p = 512 * (b - 1) + 256 * r + ridx
            length = len_ref[2 * y]
        return jnp.where(p < length, g, 0.0)

    def c_e3(b):
        return rc(I_E3 + b, SEC.at[b], GSR.at[b], PC)

    def c_e4(b):
        return rc(I_E4 + b, FP.at[b, pl.ds(2 * (1 - c), 2)], FPR.at[b, 0], PC)

    def low_rows(b, first):
        for r in range(2):
            g = SCALE * grad_rows(b, r)
            GL[r * 256 : (r + 1) * 256, :] = g.astype(BF)
            if first:
                sva[5:6, :] += jnp.sum(g, axis=0, keepdims=True)
                GLT[:, b * 512 + r * 256 : b * 512 + (r + 1) * 256] = g.T.astype(BF)

    def active_part(b, first):
        def active(n, carry):
            shard, rows = tile(n)
            g = nt(GL[...], WRED[shard, rows, :])
            g = (g * GH[b, n].astype(F32)).astype(BF)
            GH[b, n] = g
            EBA[n] += jnp.sum(g.astype(F32), axis=0, keepdims=True)
            return carry

        lax.fori_loop(first, first + 3, active, 0)

    def feed_back(b):
        low_rows(b, False)
        active_part(b, 3)

        def second(m, carry):
            rows = pl.ds(pl.multiple_of(m * 256, 256), 256)
            acc = None
            for n in range(6):
                part = nt(GH[b, n], WEXP[n // 3, rows, (n % 3) * 256 : (n % 3 + 1) * 256])
                acc = part if acc is None else acc + part
            SEC[b, :, rows] = acc.astype(BF)
            return carry

        lax.fori_loop(0, 3, second, 0)
        c_e3(b).start()

    def feed_forward(b):
        def feed(m, carry):
            cols = pl.ds(pl.multiple_of(m * 256, 256), 256)
            acc = None
            for n in range(6):
                part = nn(ACT[b, n], WRED[n // 3, (n % 3) * 256 : (n % 3 + 1) * 256, cols])
                acc = part if acc is None else acc + part
            FP[b, :, :, cols] = acc.astype(BF).reshape(4, 128, 256)
            return carry

        lax.fori_loop(0, 3, feed, 0)
        c_e4(b).start()

    def out_rows(b, yy, cc):
        if b == 0:
            return block_out.at[pl.ds(4 + 2 * cc, 2), yy]
        return block_out.at[pl.ds(8 * yy + 2 * (b - 1) + cc, 1)]

    def bo_src(b):
        return FPR.at[0, 0] if b == 0 else FPR.at[b]

    def c_e5(b):
        return rc(I_E5 + b, bo_src(b), out_rows(b, y, c), PY)

    def c_e6(b):
        return rc(I_E6 + b, bo_src(b), out_rows(b, y, c), PC)

    def c_ef(b):
        return rc(I_EF + b, out_rows(b, 1 - y, c), out_rows(b, 1 - y, c), PC)

    def l_bo(b):
        return lc(12 + b, bo_src(b), out_rows(b, y, c))

    def finish_out(b):
        c_e4(b).wait_recv()
        two = pl.ds(2 * c, 2)
        v = MID[b, two] + SCALE * (FP[b, two].astype(F32) + FPR[b, 0].astype(F32) + rbias)
        FPR[b, 0] = v.astype(BF)
        c_e5(b).start()
        c_e6(b).start()
        l_bo(b).start()

    c_e7 = rc(I_E7, GAS0.at[1], do_out.at[0, :, y], PY)

    def l_ga(b):
        if b == 0:
            return [lc(15, GAS0.at[0], do_out.at[0, :, y])]
        two = pl.ds(2 * (b - 1), 2)
        return [lc(15 + b, GAS1.at[b - 1, 0], do_out.at[1, two]), lc(17 + b, GAS1.at[b - 1, 1], do_out.at[2, two])]

    def l_gm(b):
        return lc(20 + b, MID.at[b], gm_out.at[b])

    def middle_back(b):
        c_e3(b).wait_recv()
        for r in range(2):
            rows = slice(r * 256, (r + 1) * 256)
            g = SEC[b, rows, :].astype(F32) + GSR[b, rows, :].astype(F32)
            n, rstd = stats(MID[b, 2 * r : 2 * r + 2].reshape(256, D))
            sva[3:4, :] += jnp.sum(g * n, axis=0, keepdims=True)
            sva[4:5, :] += jnp.sum(g, axis=0, keepdims=True)
            gm = grad_rows(b, r) + norm_back(g, n, rstd, gain2)
            MID[b, 2 * r : 2 * r + 2] = gm.reshape(2, 128, D)
            low = SCALE * gm
            sva[2:3, :] += jnp.sum(low, axis=0, keepdims=True)
            GL[rows, :] = low.astype(BF)
            GL1T[:, b * 512 + r * 256 : b * 512 + (r + 1) * 256] = low.T.astype(BF)
        l_gm(b).start()
        for p in range(2):
            ga = nt(GL[...], WO[p]).astype(BF)
            if b == 0:
                GAS0[p] = ga.reshape(4, 128, W3)
            else:
                GAS1[b - 1, p] = ga.reshape(2, 2, 128, W3)
        if b == 0:
            c_e7.start()
        for k in l_ga(b):
            k.start()

    for b in range(3):
        hidden_part(b, 0)
    m_red.pass_again()
    m_exp.ready()
    for b in range(3):
        hidden_part(b, 3)
    m_red.ready()
    for b in range(3):
        feed_forward(b)
    for b in range(3):
        low_rows(b, True)
        active_part(b, 0)
        finish_out(b)
    feed_back(0)
    feed_back(1)
    middle_back(0)
    feed_back(2)
    middle_back(1)

    def l_ab(n, kind):
        return lc(24 + n, ABS.at[n], ab_out.at[n % 3, kind, n // 3])

    def weight_grads(kind, left, right):
        def one(n, carry):
            if kind == 1:
                l_ab(n, 0).wait()
            for m in range(2):
                acc = None
                for b in range(3):
                    part = nn(
                        left[m * 384 : (m + 1) * 384, b * 512 : (b + 1) * 512], right[b, n]
                    )
                    acc = part if acc is None else acc + part
                ABS[n, 4 * m : 4 * m + 4] = acc.astype(BF).reshape(4, 96, 256)
            l_ab(n, kind).start()
            return carry

        lax.fori_loop(0, 6, one, 0)

    weight_grads(0, SECT, GH)
    middle_back(2)
    weight_grads(1, GLT, ACT)
    for b in range(2):
        c_e5(b).wait_recv()
        c_ef(b).start()
    for p in range(2):
        for m in range(2):
            acc = None
            for b in range(3):
                part = nn(
                    GL1T[m * 384 : (m + 1) * 384, b * 512 : (b + 1) * 512],
                    AF[p, b].reshape(512, W3),
                )
                acc = part if acc is None else acc + part
            cg_out[p, 4 * m : 4 * m + 4] = acc.astype(BF).reshape(4, 96, W3)
    for n in range(6):
        at = pl.ds(8 + (t if n < 3 else 2 * (1 - y) + c), 1)
        sva[at, (n % 3) * 256 : (n % 3 + 1) * 256] = EBA[n]

    c_e5(2).wait_recv()
    c_ef(2).start()

    for m in (m_in, m_wo, m_exp, m_red):
        m.close()
    for k in (c_sv, c_wo1, c_wo2, c_e1, c_e7):
        k.wait_send()
    c_e7.wait_recv()
    for b in range(3):
        for k in (c_e2(b, 0), c_e2(b, 1), c_e3(b), c_e4(b), c_e5(b)):
            k.wait_send()
        c_e6(b).wait()
        c_ef(b).wait()
        l_bo(b).wait()
        l_gm(b).wait()
        for k in l_ga(b):
            k.wait()
    winr.wait()
    for k in save_att:
        k.wait()
    for u in range(1, 3):
        for k in save_unit(u):
            k.wait()
    for n in range(6):
        l_ab(n, 1).wait()


def call_one(*args):
    any_ = pl.BlockSpec(memory_space=pl.ANY)
    vm = pl.BlockSpec(memory_space=pltpu.VMEM)
    sm = pl.BlockSpec(memory_space=pltpu.SMEM)
    S = jax.ShapeDtypeStruct
    outs = [
        (S((12, 2, 128, D), BF), any_),
        (S((3, 3, 4, 256, W3), BF), any_),
        (S((3, 8, 1024), F32), vm),
        (S((3, 2, 2, 2, 128, W3), BF), any_),
        (S((3, 4, 2, 128, W3), BF), any_),
        (S((3, 4, 128, D), F32), any_),
        (S((3 * W3, D), BF), any_),
        (S((3, 2, 2, 8, 96, 256), BF), any_),
        (S((2, 8, 96, W3), BF), vm),
        (S((16, D), F32), vm),
    ]
    V = pltpu.VMEM
    scratch = [
        V((2, 4, 2, 128, D), BF),
        V((4, 128, D), BF),
        V((4, 2, 128, D), BF),
        V((2, 3 * W3, D), BF),
        V((4, W3, D), BF),
        V((2, D, D), BF),
        V((2, D, D), BF),
        V((2, 8, D), F32),
        V((4, 256, D), BF),
        V((2, 4, 256, W3), BF),
        V((2, 4, 256, W3), BF),
        V((2, 4, 256, W3), BF),
        V((W3, 1024), BF),
        V((4, 4, 2, 2, 128, W3), BF),
        V((3, 4, 128, D), F32),
        V((3, 512, D), BF),
        V((D, 1536), BF),
        V((512, D), BF),
        V((D, 1536), BF),
        V((D, 1536), BF),
        V((3, 6, 512, 256), BF),
        V((3, 6, 512, 256), BF),
        V((3, 512, D), BF),
        V((3, 4, 128, D), BF),
        V((3, 1, 2, 128, D), BF),
        V((2, 4, 128, W3), BF),
        V((2, 2, 2, 2, 128, W3), BF),
        V((6, 1, 256), F32),
        V((6, 8, 96, 256), BF),
        pltpu.SemaphoreType.DMA((46,)),
        pltpu.SemaphoreType.DMA((46,)),
        pltpu.SemaphoreType.DMA((37,)),
    ]
    return pl.pallas_call(
        kernel_one,
        out_shape=[o for o, _ in outs],
        in_specs=[sm] + [any_] * 6 + [vm] * 8,
        out_specs=[s for _, s in outs],
        scratch_shapes=scratch,
        compiler_params=pltpu.CompilerParams(
            collective_id=0, has_side_effects=True, vmem_limit_bytes=VMEM_LIMIT
        ),
    )(*args)


ORDERS = ("y102", "012y", "10y2", "10y2", "y0z", "0zy", "z0y")
COLS = (256, 256, 256, W3, 256, 256, 64)


def ways(axis):
    return 4 if axis == "z" else 2


def set_shapes(index):
    lead = (2,) if index < 3 else ()
    tail = (96, COLS[index])
    axes = ["y", "2", "1", "0"]
    shapes = [lead + (2,) * 4 + tail]
    places = []
    for axis in ORDERS[index]:
        at = axes.index("2" if axis == "z" else axis)
        del axes[at : at + ways(axis) // 2]
        places.append(len(lead) + at)
        shapes.append(lead + (2,) * len(axes) + tail)
    return shapes, places


def sum_phases(n_dp):
    bits = [1 << k for k in range(n_dp.bit_length() - 1)]
    rest = bits[1:]
    return [("c",), ("y", bits[0])] + [tuple(rest[k : k + 2]) for k in range(0, len(rest), 2)]


def kernel_two(
    n_dp, len_ref, tok, qkv, lse, att, do, gm, win, winr, ab, cg, sva, g1, s1,
    tok_grad, a_out, b_out, c_out, d_out, vec_out, eb_out, qv_out,
    TOK, QS, KS, VS, AT, DO, GM, WIN, NRMT, KT, DEL, DQT, DP, QVB, GN, GNR, GNS, GNSR, SHS, SHR, TG, TGS,
    ACCW, DW0, DW1, DW2, SVR, SVC, *rest,
):
    ssem, rsem, lsem = rest[-3:]
    bufs = rest[:-3]
    dp = lax.axis_index("dp")
    t = lax.axis_index("tensor")
    y = t // 2
    c = t % 2
    PY = (dp, 2 * (1 - y) + c)
    PC = (dp, 2 * y + 1 - c)
    low = n_dp // 4
    mine = {"y": 0, "z": dp // low}
    stride = {"2": n_dp // 2, "1": n_dp // 4, "0": n_dp // 8}
    for a, v in stride.items():
        mine[a] = (dp // v) % 2

    def peer(axis, r):
        if axis == "y":
            return PY
        if axis == "z":
            return (((mine["z"] + r) % 4) * low + dp % low, t)
        return (flip(dp, stride[axis]), t)

    phases = sum_phases(n_dp)

    def sum_peer(k, mask):
        at_dp, at_t = dp, t
        for j, bit in enumerate(phases[k]):
            if (mask >> j) & 1:
                if bit == "c":
                    at_t = flip(at_t, 1)
                elif bit == "y":
                    at_t = flip(at_t, 2)
                else:
                    at_dp = flip(at_dp, bit)
        return (at_dp, at_t)

    def sum_bit(k, j):
        bit = phases[k][j]
        return c if bit == "c" else y if bit == "y" else (dp // bit) % 2

    def rc(i, src, dst, dev):
        return remote(src, dst, ssem.at[i], rsem.at[i], dev)

    def lc(i, src, dst):
        return pltpu.make_async_copy(src, dst, lsem.at[i])

    sets = []
    pos = 0
    for index in range(7):
        shapes, places = set_shapes(index)
        whole = ab.at[index] if index < 3 else (cg, DW0, DW1, DW2)[index - 3]
        steps = len(ORDERS[index])
        sums = [whole] + list(bufs[pos : pos + steps - 1])
        recvs = bufs[pos + steps - 1 : pos + 2 * steps - 1]
        pos += 2 * steps - 1
        sets.append((shapes, places, sums, recvs))

    def one_of(axis, k):
        return (k // 2, k % 2) if axis == "z" else (k,)

    def pick(ref, place, axis, k):
        return ref.at[(slice(None),) * place + one_of(axis, k)]

    def set_copies(index, step):
        shapes, places, sums, recvs = sets[index]
        order = ORDERS[index]
        axis = order[step]
        base = 5 * index + sum(ways(a) - 1 for a in order[:step])
        return [
            rc(
                base + r - 1,
                pick(sums[step], places[step], axis, (mine[axis] + r) % ways(axis)),
                recvs[step].at[r - 1],
                peer(axis, r),
            )
            for r in range(1, ways(axis))
        ]

    def set_begin(index, step):
        for k in set_copies(index, step):
            k.start()

    def keep_load(index):
        shapes, places, sums, recvs = sets[index]
        axis = ORDERS[index][0]
        return lc(20 + index, pick(sums[0], places[0], axis, mine[axis]), sums[1])

    def set_step(index, step):
        shapes, places, sums, recvs = sets[index]
        axis = ORDERS[index][step]
        for k in set_copies(index, step):
            k.wait_recv()
        in_place = index < 3 and step == 0
        if in_place:
            keep_load(index).wait()
        lead = shapes[step + 1][:-2]
        for flat in range(math.prod(lead)):
            where = []
            left = flat
            for size in reversed(lead):
                where.append(left % size)
                left //= size
            where = tuple(reversed(where))
            if in_place:
                v = sums[1][where]
            else:
                place = places[step]
                v = sums[step][where[:place] + one_of(axis, mine[axis]) + where[place:]]
            v = v.astype(F32)
            for r in range(ways(axis) - 1):
                v = v + recvs[step][(r,) + where].astype(F32)
            if step + 1 < len(ORDERS[index]):
                sums[step + 1][where] = v.astype(BF)
            elif index < 3:
                out = (a_out, b_out)[where[0]]
                out[:, index * 256 : (index + 1) * 256] = v
            elif index == 3:
                c_out[...] = v
            else:
                start = (index - 4) * 256
                d_out[:, start : start + COLS[index]] = v
        if step + 1 < len(ORDERS[index]):
            set_begin(index, step + 1)

    lds = [
        lc(0, tok.at[pl.ds(4, 4)], TOK.at[0]),
        lc(1, tok.at[pl.ds(8 * y, 4)], TOK.at[1]),
        lc(2, qkv.at[:, 0], QS),
        lc(3, qkv.at[:, 1], KS),
        lc(4, qkv.at[:, 2], VS),
        lc(5, att, AT),
        lc(6, do, DO),
        lc(7, win, WIN.at[0]),
        lc(8, winr, WIN.at[1]),
        lc(9, gm.at[0, c], GM.at[0]),
        lc(15, gm.at[pl.ds(1, 2), :, c], GM.at[pl.ds(1, 2)]),
    ]
    for k in lds:
        k.start()
    others = [(k, mask) for k in range(len(phases)) for mask in range(1, 1 << len(phases[k]))]
    greet(
        [PY, PC, peer("0", 1), peer("1", 1), peer("2", 1)]
        + [peer("z", r) for r in range(1, 4)]
        + [sum_peer(k, mask) for k, mask in others if (k, mask) not in ((0, 1), (1, 1))]
    )
    for index in range(4):
        set_begin(index, 0)
        if index < 3:
            keep_load(index).start()
    gain1 = row(g1)
    shift1 = row(s1)
    SVC[...] = sva[...]
    QVB[...] = jnp.zeros_like(QVB)
    DQT[...] = jnp.zeros_like(DQT)
    lds[0].wait()
    lds[1].wait()

    def normed(k, carry):
        n, _ = stats(TOK[k // 4, k % 4].reshape(256, D).astype(F32))
        cols = pl.ds(pl.multiple_of((k % 4) * 256, 256), 256)
        NRMT[k // 4, :, cols] = (n * gain1 + shift1).T.astype(BF)
        return carry

    lax.fori_loop(0, 8, normed, 0)
    for k in lds[2:]:
        k.wait()

    def prepare(u, carry):
        for i in range(4):
            cols = slice(i * 256, (i + 1) * 256)
            KT[u, :, cols] = KS[u, i].astype(F32).T.astype(BF)
            od = AT[u, i // 2, i % 2].reshape(256, W3).astype(F32) * DO[u, i].reshape(256, W3).astype(F32)
            DEL[u, 0:3, cols] = jnp.sum(od.T.reshape(3, HD, 256), axis=1)
        return carry

    lax.fori_loop(0, 3, prepare, 0)

    row_k = lax.broadcasted_iota(jnp.int32, (256, 256), 0)
    col_q = lax.broadcasted_iota(jnp.int32, (256, 256), 1)

    def block(u, j):
        w = u // 2
        nz = (u + 1) // 2
        length = len_ref[(1 - nz) + nz * 2 * y]
        inside = (row_k + j * 256) < length
        tiles_k, tiles_v = [], []
        for h in range(3):
            lanes = slice(h * HD, (h + 1) * HD)
            kt = head_tile(KS[u, j], h)
            vt = head_tile(VS[u, j], h)
            dk = dv = None
            for i in range(j, 4):
                cols = slice(i * 256, (i + 1) * 256)
                qh = head_tile(QS[u, i], h)
                gh = head_tile(DO[u, i].reshape(256, W3), h)
                if h < 2:
                    qh, gh = head_lanes(qh, h), head_lanes(gh, h)
                p = jnp.exp(nt(kt, qh) - lse[u, h : h + 1, cols])
                ok = inside & (row_k <= col_q) if i == j else inside
                p = jnp.where(ok, p, 0.0)
                ds = (p * (nt(vt, gh) - DEL[u, h : h + 1, cols])).astype(BF)
                pb = p.astype(BF)
                a, b = nn(pb, gh), nn(ds, qh)
                dv = a if dv is None else dv + a
                dk = b if dk is None else dk + b
                DQT[u, lanes, cols] += nn(KT[u, lanes, j * 256 : (j + 1) * 256], ds)
            tiles_k.append(dk)
            tiles_v.append(dv)
        gk = jnp.concatenate([tiles_k[0] + tiles_k[1], tiles_k[2]], axis=1)
        gv = jnp.concatenate([tiles_v[0] + tiles_v[1], tiles_v[2]], axis=1)
        gq = DQT[u, :, j * 256 : (j + 1) * 256].T * 0.125
        gq, gk, gv = gq.astype(BF), gk.astype(BF), gv.astype(BF)
        DP[u, j] = jnp.concatenate([gq, gk, gv], axis=1)
        QVB[w, 0:1, 0:W3] += jnp.sum(gq.astype(F32), axis=0, keepdims=True)
        QVB[w, 0:1, 256 : 256 + W3] += jnp.sum(gv.astype(F32), axis=0, keepdims=True)

    def finish_rows(g, x, middle):
        n, rstd = stats(x.astype(F32))
        SVC[0:1, :] += jnp.sum(g * n, axis=0, keepdims=True)
        SVC[1:2, :] += jnp.sum(g, axis=0, keepdims=True)
        return (middle + norm_back(g, n, rstd, gain1)).astype(BF)

    for j in range(4):
        block(0, j)
    for i in range(4):
        acc = nn(DP[0, i], WIN[0])
        GNS[i] = acc.astype(BF).reshape(2, 128, D)
    c_core = rc(39, GNS.at[pl.ds(2 * (1 - c), 2)], GNSR, PC)
    c_core.start()
    c_y = rc(40, SHS, SHR, PY)

    def share_rows():
        c_core.wait_recv()
        for k in range(2):
            v = GNS[2 * c + k, 1 - y].astype(F32) + GNSR[k, 1 - y].astype(F32)
            SHS[k] = v.astype(BF)
        c_y.start()

    def shared_out(yy, cc):
        return tok_grad.at[pl.ds(4 + 2 * cc, 2), yy]

    t_y = rc(53, TGS, shared_out(y, c), PY)
    t_c = rc(54, TGS, shared_out(y, c), PC)
    t_f = rc(55, shared_out(1 - y, c), shared_out(1 - y, c), PC)
    t_l = lc(10, TGS, shared_out(y, c))

    def finish_shared():
        c_y.wait_recv()
        for k in range(2):
            g = GNS[2 * c + k, y].astype(F32) + GNSR[k, y].astype(F32) + SHR[k].astype(F32)
            TGS[k] = finish_rows(g, TOK[0, 2 * c + k, y], GM[0, k])
        t_y.start()
        t_c.start()
        t_l.start()

    def c_gn(j):
        return rc(35 + j, GN.at[j, 1 - c], GNR.at[j], PC)

    def own_out(j, yy, cc):
        return tok_grad.at[8 * yy + j, cc]

    def c_own(j, k):
        if k == 0:
            return rc(41 + j, TG.at[j], own_out(j, y, c), PY)
        if k == 1:
            return rc(45 + j, TG.at[j], own_out(j, y, c), PC)
        if k == 2:
            return rc(49 + j, own_out(j, 1 - y, c), own_out(j, 1 - y, c), PC)
        return lc(11 + j, TG.at[j], own_out(j, y, c))

    def rows_back(j):
        acc = nn(DP[1, j], WIN[0]) + nn(DP[2, j], WIN[1])
        GN[j] = acc.astype(BF).reshape(2, 128, D)
        c_gn(j).start()

    def finish_own(j):
        c_gn(j).wait_recv()
        g = GN[j, c].astype(F32) + GNR[j].astype(F32)
        TG[j] = finish_rows(g, TOK[1, j, c], GM[1 + j // 2, j % 2])
        for k in (0, 1, 3):
            c_own(j, k).start()

    def pass_own(j):
        c_own(j, 0).wait_recv()
        c_own(j, 2).start()

    def input_grads(first):
        for w in range(2):
            for m in range(2):
                rows = slice(m * 384, (m + 1) * 384)
                if first:
                    acc = nn(NRMT[1, rows, 0:768], DP[1 + w, 0:3].reshape(768, 3 * W3))
                    if w == 0:
                        acc = acc + nn(NRMT[0, rows, :], DP[0].reshape(1024, 3 * W3))
                    ACCW[w, rows, :] = acc
                else:
                    acc = ACCW[w, rows, :] + nn(NRMT[1, rows, 768:1024], DP[1 + w, 3])
                    for k, ref in enumerate((DW0, DW1, DW2)):
                        cols = acc[:, 256 * k : min(256 * (k + 1), 3 * W3)]
                        ref[w, m] = cols.astype(BF).reshape(2, 2, 96, -1)

    def sum_copy(k, mask):
        return rc(
            56 + others.index((k, mask)), SVR.at[k, 0], SVR.at[k, mask], sum_peer(k, mask)
        )

    def sum_begin(k):
        for mask in range(1, 1 << len(phases[k])):
            sum_copy(k, mask).start()

    def sum_step(k):
        count = len(phases[k])
        for mask in range(1, 1 << count):
            sum_copy(k, mask).wait_recv()
        total = None
        for a in range(1 << count):
            slot = sum((((a >> j) + sum_bit(k, j)) % 2) * (1 << j) for j in range(count))
            total = SVR[k, slot] if total is None else total + SVR[k, slot]
        if k + 1 < len(phases):
            SVR[k + 1, 0] = total
            sum_begin(k + 1)
        else:
            SVC[...] = total

    def serve(step):
        for index in range(4):
            set_step(index, step)

    def own_blocks(j):
        def one(u, carry):
            block(u, j)
            if j == 0:
                pl.when(u == 1)(share_rows)
            return carry

        lax.fori_loop(1, 3, one, 0)

    own_blocks(0)
    rows_back(0)
    own_blocks(1)
    serve(0)
    finish_shared()
    finish_own(0)
    own_blocks(2)
    input_grads(True)
    own_blocks(3)
    input_grads(False)
    for index in range(4, 7):
        set_begin(index, 0)
    for j in range(1, 4):
        rows_back(j)
    t_y.wait_recv()
    t_f.start()
    pass_own(0)
    for j in range(1, 4):
        finish_own(j)
    for w in range(2):
        SVC[pl.ds(12 + (t if w == 0 else 2 * (1 - y) + c), 1), :] = QVB[w]
    SVR[0, 0] = SVC[...]
    sum_begin(0)
    serve(1)
    sum_step(0)
    for index in range(4, 7):
        set_step(index, 0)
    serve(2)
    pass_own(1)
    for index in range(4, 7):
        set_step(index, 1)
    sum_step(1)
    pass_own(2)
    serve(3)
    for index in range(4, 7):
        set_step(index, 2)
    pass_own(3)
    for k in range(2, len(phases)):
        sum_step(k)
    both = lax.broadcasted_iota(jnp.int32, (8, 1), 0) >= 2
    vec_out[...] = jnp.where(both, 0.5, 1.0) * SVC[0:8, :]
    eb_out[...] = SVC[pl.ds(8 + t, 1), :]
    qv_out[...] = SVC[pl.ds(12 + t, 1), :]

    for index in range(7):
        for step in range(len(ORDERS[index])):
            for k in set_copies(index, step):
                k.wait_send()
    for k, mask in others:
        sum_copy(k, mask).wait_send()
    for j in range(4):
        c_gn(j).wait_send()
        c_own(j, 0).wait_send()
        for k in (1, 2, 3):
            c_own(j, k).wait()
    c_core.wait_send()
    c_y.wait_send()
    t_y.wait_send()
    t_c.wait()
    t_f.wait()
    t_l.wait()


def call_two(n_dp, *args):
    any_ = pl.BlockSpec(memory_space=pl.ANY)
    vm = pl.BlockSpec(memory_space=pltpu.VMEM)
    sm = pl.BlockSpec(memory_space=pltpu.SMEM)
    S = jax.ShapeDtypeStruct
    outs = [
        (S((12, 2, 128, D), BF), any_),
        (S((96, D), F32), vm),
        (S((96, D), F32), vm),
        (S((96, W3), F32), vm),
        (S((96, 3 * W3), F32), vm),
        (S((8, D), F32), vm),
        (S((1, D), F32), vm),
        (S((1, D), F32), vm),
    ]
    V = pltpu.VMEM
    phases = sum_phases(n_dp)
    sums = sum((1 << len(v)) - 1 for v in phases)
    scratch = [
        V((2, 4, 2, 128, D), BF),
        V((3, 4, 256, W3), BF),
        V((3, 4, 256, W3), BF),
        V((3, 4, 256, W3), BF),
        V((3, 2, 2, 2, 128, W3), BF),
        V((3, 4, 2, 128, W3), BF),
        V((3, 2, 128, D), F32),
        V((2, 3 * W3, D), BF),
        V((2, D, 1024), BF),
        V((3, W3, 1024), BF),
        V((3, 8, 1024), F32),
        V((3, W3, 1024), F32),
        V((3, 4, 256, 3 * W3), BF),
        V((2, 1, D), F32),
        V((4, 2, 128, D), BF),
        V((4, 128, D), BF),
        V((4, 2, 128, D), BF),
        V((2, 2, 128, D), BF),
        V((2, 128, D), BF),
        V((2, 128, D), BF),
        V((4, 128, D), BF),
        V((2, 128, D), BF),
        V((2, D, 3 * W3), F32),
        V((2, 2, 2, 2, 96, 256), BF),
        V((2, 2, 2, 2, 96, 256), BF),
        V((2, 2, 2, 2, 96, 64), BF),
        V((len(phases), 4, 16, D), F32),
        V((16, D), F32),
    ]
    for index in range(7):
        shapes, _ = set_shapes(index)
        scratch += [V(shape, BF) for shape in shapes[1:-1]]
        scratch += [V((ways(a) - 1,) + shapes[k + 1], BF) for k, a in enumerate(ORDERS[index])]
    scratch += [
        pltpu.SemaphoreType.DMA((56 + sums,)),
        pltpu.SemaphoreType.DMA((56 + sums,)),
        pltpu.SemaphoreType.DMA((23,)),
    ]
    return pl.pallas_call(
        functools.partial(kernel_two, n_dp),
        out_shape=[o for o, _ in outs],
        in_specs=[sm, any_, any_, vm] + [any_] * 6 + [vm] * 4,
        out_specs=[s for _, s in outs],
        scratch_shapes=scratch,
        compiler_params=pltpu.CompilerParams(
            collective_id=1, has_side_effects=True, vmem_limit_bytes=VMEM_LIMIT
        ),
    )(*args)


def kernel_three(
    block_in, tok_in, a_in, b_in, c_in, d_in, rep, eb, qv,
    block_out, tok_out, a_out, b_out, c_out, d_out, v0, v1, v2, v3, v4, v5, e_out, q_out,
    hold, sem,
):
    moves = []
    for k in range(6):
        part = pl.ds(2 * k, 2)
        for j, (src, dst) in enumerate(((block_in, block_out), (tok_in, tok_out))):
            load = pltpu.make_async_copy(src.at[part], hold.at[j, part], sem.at[0, j, k])
            store = pltpu.make_async_copy(hold.at[j, part], dst.at[part], sem.at[1, j, k])
            load.start()
            moves.append((load, store))
    a_out[...] = a_in[...]
    b_out[...] = b_in[...]
    c_out[...] = c_in[...].T
    for j in range(3):
        d_out[j] = d_in[:, j * W3 : (j + 1) * W3]
    for k, ref in enumerate((v0, v1, v2, v3, v4, v5)):
        ref[...] = rep[k : k + 1, :].reshape(D)
    e_out[...] = eb[...].reshape(D)
    q_out[0:1, :] = qv[:, 0:W3]
    q_out[1:2, :] = qv[:, 256 : 256 + W3]
    for load, store in moves:
        load.wait()
        store.start()
    for load, store in moves:
        store.wait()


def call_three(*args):
    part = pl.BlockSpec(memory_space=pl.ANY)
    vm = pl.BlockSpec(memory_space=pltpu.VMEM)
    S = jax.ShapeDtypeStruct
    outs = [S((12, 2, 128, D), BF)] * 2 + [S((96, D), F32)] * 2
    outs += [S((W3, 96), F32), S((3, 96, W3), F32)] + [S((D,), F32)] * 7 + [S((2, W3), F32)]
    return pl.pallas_call(
        kernel_three,
        out_shape=outs,
        in_specs=[part] * 2 + [vm] * 7,
        out_specs=[part] * 2 + [vm] * 12,
        scratch_shapes=[pltpu.VMEM((2, 12, 2, 128, D), BF), pltpu.SemaphoreType.DMA((2, 2, 6))],
        compiler_params=pltpu.CompilerParams(vmem_limit_bytes=VMEM_LIMIT),
    )(*args)


def body(
    n_dp, tokens, lengths, first_gain, first_shift, input_weight, query_value_bias, output_weight,
    output_bias, second_gain, second_shift, expand_weight, expand_bias, reduce_weight, reduce_bias,
    cotangent,
):
    tok = tokens.reshape(12, 2, 128, D)
    cot = cotangent.reshape(12, 2, 128, D)
    win = jnp.transpose(input_weight, (1, 2, 0)).reshape(3 * W3, D)
    block_out, qkv, lse, att, do, gm, winr, ab, cg, sva = call_one(
        lengths, tok, cot, win, output_weight, expand_weight, reduce_weight, first_gain, first_shift,
        output_bias, second_gain, second_shift, reduce_bias, expand_bias, query_value_bias,
    )
    found = call_two(
        n_dp, lengths, tok, qkv, lse, att, do, gm.reshape(3, 2, 2, 128, D), win, winr,
        ab.reshape(3, 2, 2, 2, 2, 2, 96, 256), cg.reshape(2, 2, 2, 2, 96, W3), sva, first_gain, first_shift,
    )
    block_out, tok_grad, a, b, cc, d, v0, v1, v2, v3, v4, v5, eb, qv = call_three(block_out, *found)
    left = n_dp // 8
    if left > 1:
        groups = [list(range(k * left, (k + 1) * left)) for k in range(8)]
        a, b, cc, d = [
            lax.psum_scatter(v, "dp", scatter_dimension=at, axis_index_groups=groups, tiled=True)
            for v, at in ((a, 0), (b, 0), (cc, 1), (d, 1))
        ]
    return (
        block_out.reshape(tokens.shape),
        tok_grad.reshape(tokens.shape),
        v0,
        v1,
        jnp.transpose(d, (1, 0, 2)),
        qv,
        cc,
        v2,
        v3,
        v4,
        a,
        eb,
        b.T,
        v5,
    )


def solution(mesh):
    return jax.shard_map(
        functools.partial(body, mesh.shape["dp"]),
        mesh=mesh,
        in_specs=(
            P("dp", None),
            P("dp"),
            P(),
            P(),
            P(None, None, "tensor"),
            P(None, "tensor"),
            P("tensor", None),
            P(),
            P(),
            P(),
            P(None, "tensor"),
            P("tensor"),
            P("tensor", None),
            P(),
            P("dp", None),
        ),
        out_specs=(
            P("dp", None),
            P("dp", None),
            P(),
            P(),
            P("dp", None, "tensor"),
            P(None, "tensor"),
            P("tensor", "dp"),
            P(),
            P(),
            P(),
            P("dp", "tensor"),
            P("tensor"),
            P("tensor", "dp"),
            P(),
        ),
        check_vma=False,
    )
```

```python
import functools
import math

import jax
import jax.numpy as jnp
from jax import lax
from jax.experimental import pallas as pl
from jax.experimental.pallas import tpu as pltpu
from jax.sharding import PartitionSpec as P

MESH = pl.DeviceIdType.MESH
F32 = jnp.float32
BF = jnp.bfloat16
D = 768
W3 = 192
HD = 64
EPS = 1e-05
MASKED = -1e30
SCALE = 1.0 / math.sqrt(24.0)
VMEM_LIMIT = 65280 * 1024


def nn(a, b):
    return lax.dot_general(a, b, (((1,), (0,)), ((), ())), preferred_element_type=F32)


def nt(a, b):
    return lax.dot_general(a, b, (((1,), (1,)), ((), ())), preferred_element_type=F32)


def remote(src, dst, ssem, rsem, dev):
    return pltpu.make_async_remote_copy(
        src_ref=src, dst_ref=dst, send_sem=ssem, recv_sem=rsem, device_id=dev, device_id_type=MESH
    )


def flip(i, stride):
    return i + stride * (1 - 2 * ((i // stride) % 2))


def greet(peers):
    barrier = pltpu.get_barrier_semaphore()
    for peer in peers:
        pl.semaphore_signal(barrier, inc=1, device_id=peer, device_id_type=MESH)
    pl.semaphore_wait(barrier, len(peers))


def stats(v):
    mean = jnp.mean(v, axis=-1, keepdims=True)
    centre = v - mean
    rstd = lax.rsqrt(jnp.mean(centre * centre, axis=-1, keepdims=True) + EPS)
    return centre * rstd, rstd


def norm_back(grad, n, rstd, gain):
    e = grad * gain
    return rstd * (
        e - jnp.mean(e, axis=-1, keepdims=True) - n * jnp.mean(e * n, axis=-1, keepdims=True)
    )


def row(ref):
    return ref[...].astype(F32).reshape(1, D)


def head_lanes(tile, h):
    lane = lax.broadcasted_iota(jnp.int32, tile.shape, 1)
    keep = (lane < HD) if h % 2 == 0 else (lane >= HD)
    return jnp.where(keep, tile, jnp.zeros_like(tile))


def head_tile(x, h):
    return x[:, :128] if h < 2 else x[:, 128:192]


def gelu_both(v):
    c = math.sqrt(2.0 / math.pi)
    sq = v * v
    t = jnp.tanh(c * v * (1.0 + 0.044715 * sq))
    half = 0.5 * (1.0 + t)
    slope = half + (0.5 * c) * v * (1.0 - t * t) * (1.0 + (3.0 * 0.044715) * sq)
    return v * half, slope


def kernel_one(
    len_ref, tok, cot, win, wo, wexp, wred, g1, s1, ob, g2, s2, rb, eb, qvb,
    block_out, qkv_out, lse_out, att_out, do_out, gm_out, winr_out, ab_out, cg_out, sva,
    TOK, COT0, COT1, WIN, WO, WEXP, WRED, SV, NRM, QS, KS, VS, VT, AF, MID, SEC, SECT, GL, GLT, GL1T,
    ACT, GH, GSR, FP, FPR, GAS0, GAS1, EBA, ABS, ssem, rsem, lsem,
):
    dp = lax.axis_index("dp")
    t = lax.axis_index("tensor")
    y = t // 2
    c = t % 2
    PY = (dp, 2 * (1 - y) + c)
    PC = (dp, 2 * y + 1 - c)
    PX = (flip(dp, 1), t)
    PZ = (flip(dp, 2), t)
    bx = dp % 2
    bz = (dp // 2) % 2

    def rc(i, src, dst, dev):
        return remote(src, dst, ssem.at[i], rsem.at[i], dev)

    def lc(i, src, dst):
        return pltpu.make_async_copy(src, dst, lsem.at[i])

    class Spread:
        def __init__(self, base, src, full, rows, first):
            self.base, self.src, self.full, self.rows, self.first = base, src, full, rows // 4, first

        def part(self, ref, quarter, start=0, size=None):
            return ref.at[pl.ds(pl.multiple_of(quarter * self.rows + start, 16), size or self.rows)]

        def copy(self, kind):
            q, qx, qz = 2 * bx + bz, 2 * (1 - bx) + bz, 2 * bx + 1 - bz
            f, s = self.first, self.rows - self.first
            i = self.base + "yxzab".index(kind)
            if kind == "y":
                return rc(i, self.part(self.src, q), self.part(self.full, q), PY)
            if kind in "xz":
                return rc(
                    i, self.part(self.full, q), self.part(self.full, q), PX if kind == "x" else PZ
                )
            if kind == "a" and f == 0:
                q = 3 - q
                return rc(i, self.part(self.src, q), self.part(self.full, q), PY)
            if kind == "a":
                return rc(i, self.part(self.full, qz, 0, f), self.part(self.full, qz, 0, f), PX)
            return rc(i, self.part(self.full, qx, f, s), self.part(self.full, qx, f, s), PZ)

        def begin(self):
            self.copy("y").start()

        def pass_on(self):
            self.copy("y").wait_recv()
            self.copy("x").start()
            self.copy("z").start()
            if self.first == 0:
                self.copy("a").start()

        def pass_again(self):
            self.copy("x").wait_recv()
            self.copy("z").wait_recv()
            self.copy("a").start()
            self.copy("b").start()

        def ready(self):
            for kind in "xza" if self.first == 0 else "ab":
                self.copy(kind).wait_recv()

        def close(self):
            for kind in "yxza" if self.first == 0 else "yxzab":
                self.copy(kind).wait_send()

    m_in = Spread(0, win, WIN.at[1], 3 * W3, 0)
    m_wo = Spread(5, wo, WO.at[1], W3, 0)
    m_exp = Spread(10, wexp, WEXP.at[1], D, 96)
    m_red = Spread(15, wred, WRED.at[1], D, 96)
    I_SV, I_WO1, I_WO2, I_E1, I_E7 = 20, 21, 22, 23, 24
    I_E2, I_E3, I_E4, I_E5, I_E6, I_EF = 25, 31, 34, 37, 40, 43

    ld_tok = [lc(0, tok.at[pl.ds(4, 4)], TOK.at[0]), lc(1, tok.at[pl.ds(8 * y, 4)], TOK.at[1])]
    ld_win = lc(2, win, WIN.at[0])
    ld_rest = [
        lc(3, wo, WO.at[0]),
        lc(4, wexp, WEXP.at[0]),
        lc(5, wred, WRED.at[0]),
        lc(6, cot.at[pl.ds(4, 4), y], COT0),
        lc(7, cot.at[pl.ds(8 * y, 4)], COT1),
    ]
    ld_tok[0].start()
    ld_win.start()
    SV[0] = jnp.zeros((8, D), F32)
    SV[0, 0:1, :] = row(eb)
    SV[0, 1:3, 0:W3] = qvb[...].astype(F32)

    greet([PY, PC, PX, PZ])
    c_sv = rc(I_SV, SV.at[0], SV.at[1], PY)
    c_sv.start()
    m_in.begin()
    m_wo.begin()
    c_wo1 = rc(I_WO1, wo, WO.at[2], PC)
    c_wo1.start()
    ld_tok[1].start()
    for k in ld_rest:
        k.start()
    sva[...] = jnp.zeros_like(sva)
    EBA[...] = jnp.zeros_like(EBA)

    gain1, shift1 = row(g1), row(s1)
    obias, gain2, shift2, rbias = row(ob), row(g2), row(s2), row(rb)

    c_e1 = rc(I_E1, AF.at[0, 3], AF.at[1, 0], PY)

    def c_e2(b, p):
        return rc(I_E2 + 2 * b + p, AF.at[p, b], AF.at[2 + p, b], PC)

    row_k = lax.broadcasted_iota(jnp.int32, (256, 256), 0)
    col_q = lax.broadcasted_iota(jnp.int32, (256, 256), 1)

    def save_unit(u):
        return [
            lc(8 + j + 26 * (u % 2), ref.at[u % 2], qkv_out.at[u, j])
            for j, ref in enumerate((QS, KS, VS))
        ]

    def unit(u, carry):
        nz = (u + 1) // 2
        w = u // 2
        length = len_ref[(1 - nz) + nz * 2 * y]

        @pl.when(u == 0)
        def _():
            ld_tok[0].wait()

        @pl.when(u == 1)
        def _():
            ld_tok[1].wait()

        @pl.when(u < 2)
        def _():
            for i in range(4):
                n, _ = stats(TOK[u, i].reshape(256, D).astype(F32))
                NRM[i] = (n * gain1 + shift1).astype(BF)

        @pl.when(u == 0)
        def _():
            ld_win.wait()

        @pl.when(u == 2)
        def _():
            for k in save_unit(0):
                k.wait()
            m_in.ready()
            c_sv.wait_recv()

        for i in range(4):
            x = NRM[i]
            q = nt(x, WIN[w, 0:W3, :]) + SV[w, 1:2, 0:W3]
            QS[u % 2, i] = q.astype(BF) * jnp.asarray(0.125, BF)
            k = nt(x, WIN[w, W3 : 2 * W3, :])
            KS[u % 2, i] = k.astype(BF)
            v = nt(x, WIN[w, 2 * W3 : 3 * W3, :]) + SV[w, 2:3, 0:W3]
            VS[u % 2, i] = v.astype(BF)
            VT[:, i * 256 : (i + 1) * 256] = v.T.astype(BF)
        for k in save_unit(u):
            k.start()

        for i in range(4):
            qi = QS[u % 2, i]
            outs = []
            for h in range(3):
                qh = head_tile(qi, h)
                if h < 2:
                    qh = head_lanes(qh, h)
                parts = []
                for kb in range(i + 1):
                    s = nt(head_tile(KS[u % 2, kb], h), qh)
                    ok = (row_k + kb * 256) < length
                    if kb == i:
                        ok = ok & (row_k <= col_q)
                    parts.append(jnp.where(ok, s, MASKED))
                top = functools.reduce(
                    jnp.maximum, [jnp.max(s, axis=0, keepdims=True) for s in parts]
                )
                total = jnp.zeros_like(top)
                acc = jnp.zeros((HD, 256), F32)
                for kb, s in enumerate(parts):
                    p = jnp.exp(s - top)
                    total = total + jnp.sum(p, axis=0, keepdims=True)
                    acc = acc + nn(
                        VT[h * HD : (h + 1) * HD, kb * 256 : (kb + 1) * 256], p.astype(BF)
                    )
                outs.append(acc * (1.0 / total))
                lse_out[u, h : h + 1, i * 256 : (i + 1) * 256] = top + jnp.log(total)
            o = jnp.concatenate(outs, axis=0).T.astype(BF)
            for hh in range(2):
                blk = (1 - nz) * (3 * ((hh + y) % 2)) + nz * (1 + i // 2)
                s0 = (1 - nz) * (i // 2) + nz * (i % 2)
                s1 = (1 - nz) * (i % 2) + nz * hh
                AF[w, blk, s0, s1] = o[hh * 128 : (hh + 1) * 128]

            if i == 1:

                @pl.when(u == 1)
                def _():
                    m_exp.begin()

                @pl.when(u == 2)
                def _():
                    c_e2(1, 1).start()

        @pl.when(u == 0)
        def _():
            m_in.pass_on()
            c_e2(0, 0).start()

        @pl.when(u == 1)
        def _():
            m_wo.pass_on()
            c_e1.start()
            m_red.begin()
            c_e2(1, 0).start()
            c_e2(2, 0).start()

        @pl.when(u == 2)
        def _():
            c_e2(2, 1).start()

        return carry

    lax.fori_loop(0, 3, unit, 0)
    save_att = [
        lc(30, AF.at[0, 0], att_out.at[0, :, :, y]),
        lc(31, AF.at[0, 3], att_out.at[0, :, :, 1 - y]),
        lc(32, AF.at[0, pl.ds(1, 2)], att_out.at[1]),
        lc(33, AF.at[1, pl.ds(1, 2)], att_out.at[2]),
    ]
    for k in save_att:
        k.start()
    m_exp.pass_on()
    m_wo.ready()
    c_wo2 = rc(I_WO2, WO.at[1], WO.at[3], PC)
    c_wo2.start()
    winr = lc(11, WIN.at[1], winr_out)
    winr.start()
    for k in ld_rest:
        k.wait()
    c_wo1.wait_recv()
    c_wo2.wait_recv()

    def tok_rows(b, r):
        if b == 0:
            v = jnp.concatenate([TOK[0, 2 * r, y], TOK[0, 2 * r + 1, y]], axis=0)
        else:
            v = TOK[1, 2 * (b - 1) + r].reshape(256, D)
        return v.astype(F32)

    for b in (1, 2, 0):
        for p in range(2):
            c_e2(b, p).wait_recv()
        for r in range(2):
            acc = None
            for p in range(4):
                part = nn(AF[p, b, r].reshape(256, W3), WO[p])
                acc = part if acc is None else acc + part
            mid = tok_rows(b, r) + SCALE * (acc + obias)
            MID[b, 2 * r : 2 * r + 2] = mid.reshape(2, 128, D)
            n, _ = stats(mid)
            sec = n * gain2 + shift2
            SEC[b, r * 256 : (r + 1) * 256, :] = sec.astype(BF)
            SECT[:, b * 512 + r * 256 : b * 512 + (r + 1) * 256] = sec.T.astype(BF)
        if b == 1:
            c_e1.wait_recv()
            c_e2(0, 1).start()
        if b == 2:
            m_red.pass_on()
    m_exp.pass_again()

    def tile(n):
        return n // 3, pl.ds(pl.multiple_of((n % 3) * 256, 256), 256)

    def hidden_part(b, first):
        def hidden(n, carry):
            shard, cols = tile(n)
            h = nn(SEC[b], WEXP[shard, :, cols]) + SV[shard, 0:1, cols]
            act, slope = gelu_both(h)
            ACT[b, n] = act.astype(BF)
            GH[b, n] = slope.astype(BF)
            return carry

        lax.fori_loop(first, first + 3, hidden, 0)

    ridx = lax.broadcasted_iota(jnp.int32, (256, 1), 0)

    def grad_rows(b, r):
        if b == 0:
            g = COT0[2 * r : 2 * r + 2].reshape(256, D).astype(F32)
            p = 512 * r + 256 * (ridx // 128) + 128 * y + ridx % 128
            length = len_ref[1]
        else:
            g = COT1[2 * (b - 1) + r].reshape(256, D).astype(F32)
            p = 512 * (b - 1) + 256 * r + ridx
            length = len_ref[2 * y]
        return jnp.where(p < length, g, 0.0)

    def c_e3(b):
        return rc(I_E3 + b, SEC.at[b], GSR.at[b], PC)

    def c_e4(b):
        return rc(I_E4 + b, FP.at[b, pl.ds(2 * (1 - c), 2)], FPR.at[b, 0], PC)

    def low_rows(b, first):
        for r in range(2):
            g = SCALE * grad_rows(b, r)
            GL[r * 256 : (r + 1) * 256, :] = g.astype(BF)
            if first:
                sva[5:6, :] += jnp.sum(g, axis=0, keepdims=True)
                GLT[:, b * 512 + r * 256 : b * 512 + (r + 1) * 256] = g.T.astype(BF)

    def active_part(b, first):
        def active(n, carry):
            shard, rows = tile(n)
            g = nt(GL[...], WRED[shard, rows, :])
            g = (g * GH[b, n].astype(F32)).astype(BF)
            GH[b, n] = g
            EBA[n] += jnp.sum(g.astype(F32), axis=0, keepdims=True)
            return carry

        lax.fori_loop(first, first + 3, active, 0)

    def feed_back(b):
        low_rows(b, False)
        active_part(b, 3)

        def second(m, carry):
            rows = pl.ds(pl.multiple_of(m * 256, 256), 256)
            acc = None
            for n in range(6):
                part = nt(GH[b, n], WEXP[n // 3, rows, (n % 3) * 256 : (n % 3 + 1) * 256])
                acc = part if acc is None else acc + part
            SEC[b, :, rows] = acc.astype(BF)
            return carry

        lax.fori_loop(0, 3, second, 0)
        c_e3(b).start()

    def feed_forward(b):
        def feed(m, carry):
            cols = pl.ds(pl.multiple_of(m * 256, 256), 256)
            acc = None
            for n in range(6):
                part = nn(ACT[b, n], WRED[n // 3, (n % 3) * 256 : (n % 3 + 1) * 256, cols])
                acc = part if acc is None else acc + part
            FP[b, :, :, cols] = acc.astype(BF).reshape(4, 128, 256)
            return carry

        lax.fori_loop(0, 3, feed, 0)
        c_e4(b).start()

    def out_rows(b, yy, cc):
        if b == 0:
            return block_out.at[pl.ds(4 + 2 * cc, 2), yy]
        return block_out.at[pl.ds(8 * yy + 2 * (b - 1) + cc, 1)]

    def bo_src(b):
        return FPR.at[0, 0] if b == 0 else FPR.at[b]

    def c_e5(b):
        return rc(I_E5 + b, bo_src(b), out_rows(b, y, c), PY)

    def c_e6(b):
        return rc(I_E6 + b, bo_src(b), out_rows(b, y, c), PC)

    def c_ef(b):
        return rc(I_EF + b, out_rows(b, 1 - y, c), out_rows(b, 1 - y, c), PC)

    def l_bo(b):
        return lc(12 + b, bo_src(b), out_rows(b, y, c))

    def finish_out(b):
        c_e4(b).wait_recv()
        two = pl.ds(2 * c, 2)
        v = MID[b, two] + SCALE * (FP[b, two].astype(F32) + FPR[b, 0].astype(F32) + rbias)
        FPR[b, 0] = v.astype(BF)
        c_e5(b).start()
        c_e6(b).start()
        l_bo(b).start()

    c_e7 = rc(I_E7, GAS0.at[1], do_out.at[0, :, y], PY)

    def l_ga(b):
        if b == 0:
            return [lc(15, GAS0.at[0], do_out.at[0, :, y])]
        two = pl.ds(2 * (b - 1), 2)
        return [lc(15 + b, GAS1.at[b - 1, 0], do_out.at[1, two]), lc(17 + b, GAS1.at[b - 1, 1], do_out.at[2, two])]

    def l_gm(b):
        return lc(20 + b, MID.at[b], gm_out.at[b])

    def middle_back(b):
        c_e3(b).wait_recv()
        for r in range(2):
            rows = slice(r * 256, (r + 1) * 256)
            g = SEC[b, rows, :].astype(F32) + GSR[b, rows, :].astype(F32)
            n, rstd = stats(MID[b, 2 * r : 2 * r + 2].reshape(256, D))
            sva[3:4, :] += jnp.sum(g * n, axis=0, keepdims=True)
            sva[4:5, :] += jnp.sum(g, axis=0, keepdims=True)
            gm = grad_rows(b, r) + norm_back(g, n, rstd, gain2)
            MID[b, 2 * r : 2 * r + 2] = gm.reshape(2, 128, D)
            low = SCALE * gm
            sva[2:3, :] += jnp.sum(low, axis=0, keepdims=True)
            GL[rows, :] = low.astype(BF)
            GL1T[:, b * 512 + r * 256 : b * 512 + (r + 1) * 256] = low.T.astype(BF)
        l_gm(b).start()
        for p in range(2):
            ga = nt(GL[...], WO[p]).astype(BF)
            if b == 0:
                GAS0[p] = ga.reshape(4, 128, W3)
            else:
                GAS1[b - 1, p] = ga.reshape(2, 2, 128, W3)
        if b == 0:
            c_e7.start()
        for k in l_ga(b):
            k.start()

    for b in range(3):
        hidden_part(b, 0)
    m_red.pass_again()
    m_exp.ready()
    hidden_part(0, 3)
    hidden_part(1, 3)
    m_red.ready()
    feed_forward(0)
    hidden_part(2, 3)
    feed_forward(1)
    finish_out(0)
    feed_forward(2)
    finish_out(1)
    low_rows(0, True)
    active_part(0, 0)
    finish_out(2)
    for b in range(1, 3):
        low_rows(b, True)
        active_part(b, 0)
    feed_back(0)
    feed_back(1)
    middle_back(0)
    feed_back(2)
    middle_back(1)

    def l_ab(n, kind):
        return lc(24 + n, ABS.at[n], ab_out.at[n % 3, kind, n // 3])

    def weight_grads(kind, left, right):
        def one(n, carry):
            if kind == 1:
                l_ab(n, 0).wait()
            for m in range(2):
                acc = None
                for b in range(3):
                    part = nn(
                        left[m * 384 : (m + 1) * 384, b * 512 : (b + 1) * 512], right[b, n]
                    )
                    acc = part if acc is None else acc + part
                ABS[n, 4 * m : 4 * m + 4] = acc.astype(BF).reshape(4, 96, 256)
            l_ab(n, kind).start()
            return carry

        lax.fori_loop(0, 6, one, 0)

    weight_grads(0, SECT, GH)
    middle_back(2)
    weight_grads(1, GLT, ACT)
    for b in range(2):
        c_e5(b).wait_recv()
        c_ef(b).start()
    for p in range(2):
        for m in range(2):
            acc = None
            for b in range(3):
                part = nn(
                    GL1T[m * 384 : (m + 1) * 384, b * 512 : (b + 1) * 512],
                    AF[p, b].reshape(512, W3),
                )
                acc = part if acc is None else acc + part
            cg_out[p, 4 * m : 4 * m + 4] = acc.astype(BF).reshape(4, 96, W3)
    for n in range(6):
        at = pl.ds(8 + (t if n < 3 else 2 * (1 - y) + c), 1)
        sva[at, (n % 3) * 256 : (n % 3 + 1) * 256] = EBA[n]

    c_e5(2).wait_recv()
    c_ef(2).start()

    for m in (m_in, m_wo, m_exp, m_red):
        m.close()
    for k in (c_sv, c_wo1, c_wo2, c_e1, c_e7):
        k.wait_send()
    c_e7.wait_recv()
    for b in range(3):
        for k in (c_e2(b, 0), c_e2(b, 1), c_e3(b), c_e4(b), c_e5(b)):
            k.wait_send()
        c_e6(b).wait()
        c_ef(b).wait()
        l_bo(b).wait()
        l_gm(b).wait()
        for k in l_ga(b):
            k.wait()
    winr.wait()
    for k in save_att:
        k.wait()
    for u in range(1, 3):
        for k in save_unit(u):
            k.wait()
    for n in range(6):
        l_ab(n, 1).wait()


def call_one(*args):
    any_ = pl.BlockSpec(memory_space=pl.ANY)
    vm = pl.BlockSpec(memory_space=pltpu.VMEM)
    sm = pl.BlockSpec(memory_space=pltpu.SMEM)
    S = jax.ShapeDtypeStruct
    outs = [
        (S((12, 2, 128, D), BF), any_),
        (S((3, 3, 4, 256, W3), BF), any_),
        (S((3, 8, 1024), F32), vm),
        (S((3, 2, 2, 2, 128, W3), BF), any_),
        (S((3, 4, 2, 128, W3), BF), any_),
        (S((3, 4, 128, D), F32), any_),
        (S((3 * W3, D), BF), any_),
        (S((3, 2, 2, 8, 96, 256), BF), any_),
        (S((2, 8, 96, W3), BF), vm),
        (S((16, D), F32), vm),
    ]
    V = pltpu.VMEM
    scratch = [
        V((2, 4, 2, 128, D), BF),
        V((4, 128, D), BF),
        V((4, 2, 128, D), BF),
        V((2, 3 * W3, D), BF),
        V((4, W3, D), BF),
        V((2, D, D), BF),
        V((2, D, D), BF),
        V((2, 8, D), F32),
        V((4, 256, D), BF),
        V((2, 4, 256, W3), BF),
        V((2, 4, 256, W3), BF),
        V((2, 4, 256, W3), BF),
        V((W3, 1024), BF),
        V((4, 4, 2, 2, 128, W3), BF),
        V((3, 4, 128, D), F32),
        V((3, 512, D), BF),
        V((D, 1536), BF),
        V((512, D), BF),
        V((D, 1536), BF),
        V((D, 1536), BF),
        V((3, 6, 512, 256), BF),
        V((3, 6, 512, 256), BF),
        V((3, 512, D), BF),
        V((3, 4, 128, D), BF),
        V((3, 1, 2, 128, D), BF),
        V((2, 4, 128, W3), BF),
        V((2, 2, 2, 2, 128, W3), BF),
        V((6, 1, 256), F32),
        V((6, 8, 96, 256), BF),
        pltpu.SemaphoreType.DMA((46,)),
        pltpu.SemaphoreType.DMA((46,)),
        pltpu.SemaphoreType.DMA((37,)),
    ]
    return pl.pallas_call(
        kernel_one,
        out_shape=[o for o, _ in outs],
        in_specs=[sm] + [any_] * 6 + [vm] * 8,
        out_specs=[s for _, s in outs],
        scratch_shapes=scratch,
        compiler_params=pltpu.CompilerParams(
            collective_id=0, has_side_effects=True, vmem_limit_bytes=VMEM_LIMIT
        ),
    )(*args)


ORDERS = ("y102", "012y", "10y2", "10y2", "y0z", "0zy", "z0y")
COLS = (256, 256, 256, W3, 256, 256, 64)


def ways(axis):
    return 4 if axis == "z" else 2


def set_shapes(index):
    lead = (2,) if index < 3 else ()
    tail = (96, COLS[index])
    axes = ["y", "2", "1", "0"]
    shapes = [lead + (2,) * 4 + tail]
    places = []
    for axis in ORDERS[index]:
        at = axes.index("2" if axis == "z" else axis)
        del axes[at : at + ways(axis) // 2]
        places.append(len(lead) + at)
        shapes.append(lead + (2,) * len(axes) + tail)
    return shapes, places


def sum_phases(n_dp):
    bits = [1 << k for k in range(n_dp.bit_length() - 1)]
    rest = bits[1:]
    return [("c",), ("y", bits[0])] + [tuple(rest[k : k + 2]) for k in range(0, len(rest), 2)]


def kernel_two(
    n_dp, len_ref, tok, qkv, lse, att, do, gm, win, winr, ab, cg, sva, g1, s1,
    tok_grad, a_out, b_out, c_out, d_out, vec_out, eb_out, qv_out,
    TOK, QS, KS, VS, AT, DO, GM, WIN, NRMT, KT, DEL, DQT, DP, QVB, GN, GNR, GNS, GNSR, SHS, SHR, TG, TGS,
    ACCW, DW0, DW1, DW2, SVR, SVC, *rest,
):
    ssem, rsem, lsem = rest[-3:]
    bufs = rest[:-3]
    dp = lax.axis_index("dp")
    t = lax.axis_index("tensor")
    y = t // 2
    c = t % 2
    PY = (dp, 2 * (1 - y) + c)
    PC = (dp, 2 * y + 1 - c)
    low = n_dp // 4
    mine = {"y": 0, "z": dp // low}
    stride = {"2": n_dp // 2, "1": n_dp // 4, "0": n_dp // 8}
    for a, v in stride.items():
        mine[a] = (dp // v) % 2

    def peer(axis, r):
        if axis == "y":
            return PY
        if axis == "z":
            return (((mine["z"] + r) % 4) * low + dp % low, t)
        return (flip(dp, stride[axis]), t)

    phases = sum_phases(n_dp)

    def sum_peer(k, mask):
        at_dp, at_t = dp, t
        for j, bit in enumerate(phases[k]):
            if (mask >> j) & 1:
                if bit == "c":
                    at_t = flip(at_t, 1)
                elif bit == "y":
                    at_t = flip(at_t, 2)
                else:
                    at_dp = flip(at_dp, bit)
        return (at_dp, at_t)

    def sum_bit(k, j):
        bit = phases[k][j]
        return c if bit == "c" else y if bit == "y" else (dp // bit) % 2

    def rc(i, src, dst, dev):
        return remote(src, dst, ssem.at[i], rsem.at[i], dev)

    def lc(i, src, dst):
        return pltpu.make_async_copy(src, dst, lsem.at[i])

    sets = []
    pos = 0
    for index in range(7):
        shapes, places = set_shapes(index)
        whole = ab.at[index] if index < 3 else (cg, DW0, DW1, DW2)[index - 3]
        steps = len(ORDERS[index])
        sums = [whole] + list(bufs[pos : pos + steps - 1])
        recvs = bufs[pos + steps - 1 : pos + 2 * steps - 1]
        pos += 2 * steps - 1
        sets.append((shapes, places, sums, recvs))

    def one_of(axis, k):
        return (k // 2, k % 2) if axis == "z" else (k,)

    def pick(ref, place, axis, k):
        return ref.at[(slice(None),) * place + one_of(axis, k)]

    def set_copies(index, step):
        shapes, places, sums, recvs = sets[index]
        order = ORDERS[index]
        axis = order[step]
        base = 5 * index + sum(ways(a) - 1 for a in order[:step])
        return [
            rc(
                base + r - 1,
                pick(sums[step], places[step], axis, (mine[axis] + r) % ways(axis)),
                recvs[step].at[r - 1],
                peer(axis, r),
            )
            for r in range(1, ways(axis))
        ]

    def set_begin(index, step):
        for k in set_copies(index, step):
            k.start()

    def keep_load(index):
        shapes, places, sums, recvs = sets[index]
        axis = ORDERS[index][0]
        return lc(20 + index, pick(sums[0], places[0], axis, mine[axis]), sums[1])

    def set_step(index, step):
        shapes, places, sums, recvs = sets[index]
        axis = ORDERS[index][step]
        for k in set_copies(index, step):
            k.wait_recv()
        in_place = index < 3 and step == 0
        if in_place:
            keep_load(index).wait()
        lead = shapes[step + 1][:-2]
        for flat in range(math.prod(lead)):
            where = []
            left = flat
            for size in reversed(lead):
                where.append(left % size)
                left //= size
            where = tuple(reversed(where))
            if in_place:
                v = sums[1][where]
            else:
                place = places[step]
                v = sums[step][where[:place] + one_of(axis, mine[axis]) + where[place:]]
            v = v.astype(F32)
            for r in range(ways(axis) - 1):
                v = v + recvs[step][(r,) + where].astype(F32)
            if step + 1 < len(ORDERS[index]):
                sums[step + 1][where] = v.astype(BF)
            elif index < 3:
                out = (a_out, b_out)[where[0]]
                out[:, index * 256 : (index + 1) * 256] = v
            elif index == 3:
                c_out[...] = v
            else:
                start = (index - 4) * 256
                d_out[:, start : start + COLS[index]] = v
        if step + 1 < len(ORDERS[index]):
            set_begin(index, step + 1)

    lds = [
        lc(0, tok.at[pl.ds(4, 4)], TOK.at[0]),
        lc(1, tok.at[pl.ds(8 * y, 4)], TOK.at[1]),
        lc(2, qkv.at[:, 0], QS),
        lc(3, qkv.at[:, 1], KS),
        lc(4, qkv.at[:, 2], VS),
        lc(5, att, AT),
        lc(6, do, DO),
        lc(7, win, WIN.at[0]),
        lc(8, winr, WIN.at[1]),
        lc(9, gm.at[0, c], GM.at[0]),
        lc(15, gm.at[pl.ds(1, 2), :, c], GM.at[pl.ds(1, 2)]),
    ]
    for k in lds:
        k.start()
    others = [(k, mask) for k in range(len(phases)) for mask in range(1, 1 << len(phases[k]))]
    greet(
        [PY, PC, peer("0", 1), peer("1", 1), peer("2", 1)]
        + [peer("z", r) for r in range(1, 4)]
        + [sum_peer(k, mask) for k, mask in others if (k, mask) not in ((0, 1), (1, 1))]
    )
    for index in range(4):
        set_begin(index, 0)
        if index < 3:
            keep_load(index).start()
    gain1 = row(g1)
    shift1 = row(s1)
    SVC[...] = sva[...]
    QVB[...] = jnp.zeros_like(QVB)
    DQT[...] = jnp.zeros_like(DQT)
    lds[0].wait()
    lds[1].wait()

    def normed(k, carry):
        n, _ = stats(TOK[k // 4, k % 4].reshape(256, D).astype(F32))
        cols = pl.ds(pl.multiple_of((k % 4) * 256, 256), 256)
        NRMT[k // 4, :, cols] = (n * gain1 + shift1).T.astype(BF)
        return carry

    lax.fori_loop(0, 8, normed, 0)
    for k in lds[2:]:
        k.wait()

    def prepare(u, carry):
        for i in range(4):
            cols = slice(i * 256, (i + 1) * 256)
            KT[u, :, cols] = KS[u, i].astype(F32).T.astype(BF)
            od = AT[u, i // 2, i % 2].reshape(256, W3).astype(F32) * DO[u, i].reshape(256, W3).astype(F32)
            DEL[u, 0:3, cols] = jnp.sum(od.T.reshape(3, HD, 256), axis=1)
        return carry

    lax.fori_loop(0, 3, prepare, 0)

    row_k = lax.broadcasted_iota(jnp.int32, (256, 256), 0)
    col_q = lax.broadcasted_iota(jnp.int32, (256, 256), 1)

    def block(u, j):
        w = u // 2
        nz = (u + 1) // 2
        length = len_ref[(1 - nz) + nz * 2 * y]
        inside = (row_k + j * 256) < length
        tiles_k, tiles_v = [], []
        for h in range(3):
            lanes = slice(h * HD, (h + 1) * HD)
            kt = head_tile(KS[u, j], h)
            vt = head_tile(VS[u, j], h)
            dk = dv = None
            for i in range(j, 4):
                cols = slice(i * 256, (i + 1) * 256)
                qh = head_tile(QS[u, i], h)
                gh = head_tile(DO[u, i].reshape(256, W3), h)
                if h < 2:
                    qh, gh = head_lanes(qh, h), head_lanes(gh, h)
                p = jnp.exp(nt(kt, qh) - lse[u, h : h + 1, cols])
                ok = inside & (row_k <= col_q) if i == j else inside
                p = jnp.where(ok, p, 0.0)
                ds = (p * (nt(vt, gh) - DEL[u, h : h + 1, cols])).astype(BF)
                pb = p.astype(BF)
                a, b = nn(pb, gh), nn(ds, qh)
                dv = a if dv is None else dv + a
                dk = b if dk is None else dk + b
                DQT[u, lanes, cols] += nn(KT[u, lanes, j * 256 : (j + 1) * 256], ds)
            tiles_k.append(dk)
            tiles_v.append(dv)
        gk = jnp.concatenate([tiles_k[0] + tiles_k[1], tiles_k[2]], axis=1)
        gv = jnp.concatenate([tiles_v[0] + tiles_v[1], tiles_v[2]], axis=1)
        gq = DQT[u, :, j * 256 : (j + 1) * 256].T * 0.125
        gq, gk, gv = gq.astype(BF), gk.astype(BF), gv.astype(BF)
        DP[u, j] = jnp.concatenate([gq, gk, gv], axis=1)
        QVB[w, 0:1, 0:W3] += jnp.sum(gq.astype(F32), axis=0, keepdims=True)
        QVB[w, 0:1, 256 : 256 + W3] += jnp.sum(gv.astype(F32), axis=0, keepdims=True)

    def finish_rows(g, x, middle):
        n, rstd = stats(x.astype(F32))
        SVC[0:1, :] += jnp.sum(g * n, axis=0, keepdims=True)
        SVC[1:2, :] += jnp.sum(g, axis=0, keepdims=True)
        return (middle + norm_back(g, n, rstd, gain1)).astype(BF)

    for j in range(4):
        block(0, j)
    for i in range(4):
        acc = nn(DP[0, i], WIN[0])
        GNS[i] = acc.astype(BF).reshape(2, 128, D)
    c_core = rc(39, GNS.at[pl.ds(2 * (1 - c), 2)], GNSR, PC)
    c_core.start()
    c_y = rc(40, SHS, SHR, PY)

    def share_rows():
        c_core.wait_recv()
        for k in range(2):
            v = GNS[2 * c + k, 1 - y].astype(F32) + GNSR[k, 1 - y].astype(F32)
            SHS[k] = v.astype(BF)
        c_y.start()

    def shared_out(yy, cc):
        return tok_grad.at[pl.ds(4 + 2 * cc, 2), yy]

    t_y = rc(53, TGS, shared_out(y, c), PY)
    t_c = rc(54, TGS, shared_out(y, c), PC)
    t_f = rc(55, shared_out(1 - y, c), shared_out(1 - y, c), PC)
    t_l = lc(10, TGS, shared_out(y, c))

    def finish_shared():
        c_y.wait_recv()
        for k in range(2):
            g = GNS[2 * c + k, y].astype(F32) + GNSR[k, y].astype(F32) + SHR[k].astype(F32)
            TGS[k] = finish_rows(g, TOK[0, 2 * c + k, y], GM[0, k])
        t_y.start()
        t_c.start()
        t_l.start()

    def c_gn(j):
        return rc(35 + j, GN.at[j, 1 - c], GNR.at[j], PC)

    def own_out(j, yy, cc):
        return tok_grad.at[8 * yy + j, cc]

    def c_own(j, k):
        if k == 0:
            return rc(41 + j, TG.at[j], own_out(j, y, c), PY)
        if k == 1:
            return rc(45 + j, TG.at[j], own_out(j, y, c), PC)
        if k == 2:
            return rc(49 + j, own_out(j, 1 - y, c), own_out(j, 1 - y, c), PC)
        return lc(11 + j, TG.at[j], own_out(j, y, c))

    def rows_back(j):
        acc = nn(DP[1, j], WIN[0]) + nn(DP[2, j], WIN[1])
        GN[j] = acc.astype(BF).reshape(2, 128, D)
        c_gn(j).start()

    def finish_own(j):
        c_gn(j).wait_recv()
        g = GN[j, c].astype(F32) + GNR[j].astype(F32)
        TG[j] = finish_rows(g, TOK[1, j, c], GM[1 + j // 2, j % 2])
        for k in (0, 1, 3):
            c_own(j, k).start()

    def pass_own(j):
        c_own(j, 0).wait_recv()
        c_own(j, 2).start()

    def input_grads(first):
        for w in range(2):
            for m in range(2):
                rows = slice(m * 384, (m + 1) * 384)
                if first:
                    acc = nn(NRMT[1, rows, 0:768], DP[1 + w, 0:3].reshape(768, 3 * W3))
                    if w == 0:
                        acc = acc + nn(NRMT[0, rows, :], DP[0].reshape(1024, 3 * W3))
                    ACCW[w, rows, :] = acc
                else:
                    acc = ACCW[w, rows, :] + nn(NRMT[1, rows, 768:1024], DP[1 + w, 3])
                    for k, ref in enumerate((DW0, DW1, DW2)):
                        cols = acc[:, 256 * k : min(256 * (k + 1), 3 * W3)]
                        ref[w, m] = cols.astype(BF).reshape(2, 2, 96, -1)

    def sum_copy(k, mask):
        return rc(
            56 + others.index((k, mask)), SVR.at[k, 0], SVR.at[k, mask], sum_peer(k, mask)
        )

    def sum_begin(k):
        for mask in range(1, 1 << len(phases[k])):
            sum_copy(k, mask).start()

    def sum_step(k):
        count = len(phases[k])
        for mask in range(1, 1 << count):
            sum_copy(k, mask).wait_recv()
        total = None
        for a in range(1 << count):
            slot = sum((((a >> j) + sum_bit(k, j)) % 2) * (1 << j) for j in range(count))
            total = SVR[k, slot] if total is None else total + SVR[k, slot]
        if k + 1 < len(phases):
            SVR[k + 1, 0] = total
            sum_begin(k + 1)
        else:
            SVC[...] = total

    def serve(step, which=(0, 1, 2, 3)):
        for index in which:
            set_step(index, step)

    def own_blocks(j):
        def one(u, carry):
            block(u, j)
            if j == 0:
                pl.when(u == 1)(share_rows)
            return carry

        lax.fori_loop(1, 3, one, 0)

    own_blocks(0)
    rows_back(0)
    serve(0, (0, 1))
    own_blocks(1)
    serve(0, (2, 3))
    finish_shared()
    finish_own(0)
    own_blocks(2)
    input_grads(True)
    own_blocks(3)
    input_grads(False)
    for index in range(4, 7):
        set_begin(index, 0)
    for j in range(1, 4):
        rows_back(j)
    serve(1, (0, 1))
    pass_own(0)
    t_y.wait_recv()
    t_f.start()
    finish_own(1)
    serve(1, (2, 3))
    for index in (5, 6, 4):
        set_step(index, 0)
    finish_own(2)
    finish_own(3)
    for w in range(2):
        SVC[pl.ds(12 + (t if w == 0 else 2 * (1 - y) + c), 1), :] = QVB[w]
    SVR[0, 0] = SVC[...]
    sum_begin(0)
    serve(2, (0, 1))
    sum_step(0)
    serve(2, (2, 3))
    set_step(6, 1)
    set_step(4, 1)
    pass_own(1)
    sum_step(1)
    set_step(5, 1)
    serve(3)
    pass_own(2)
    set_step(6, 2)
    for k in range(2, len(phases)):
        sum_step(k)
    pass_own(3)
    set_step(5, 2)
    set_step(4, 2)
    both = lax.broadcasted_iota(jnp.int32, (8, 1), 0) >= 2
    vec_out[...] = jnp.where(both, 0.5, 1.0) * SVC[0:8, :]
    eb_out[...] = SVC[pl.ds(8 + t, 1), :]
    qv_out[...] = SVC[pl.ds(12 + t, 1), :]

    for index in range(7):
        for step in range(len(ORDERS[index])):
            for k in set_copies(index, step):
                k.wait_send()
    for k, mask in others:
        sum_copy(k, mask).wait_send()
    for j in range(4):
        c_gn(j).wait_send()
        c_own(j, 0).wait_send()
        for k in (1, 2, 3):
            c_own(j, k).wait()
    c_core.wait_send()
    c_y.wait_send()
    t_y.wait_send()
    t_c.wait()
    t_f.wait()
    t_l.wait()


def call_two(n_dp, *args):
    any_ = pl.BlockSpec(memory_space=pl.ANY)
    vm = pl.BlockSpec(memory_space=pltpu.VMEM)
    sm = pl.BlockSpec(memory_space=pltpu.SMEM)
    S = jax.ShapeDtypeStruct
    outs = [
        (S((12, 2, 128, D), BF), any_),
        (S((96, D), F32), vm),
        (S((96, D), F32), vm),
        (S((96, W3), F32), vm),
        (S((96, 3 * W3), F32), vm),
        (S((8, D), F32), vm),
        (S((1, D), F32), vm),
        (S((1, D), F32), vm),
    ]
    V = pltpu.VMEM
    phases = sum_phases(n_dp)
    sums = sum((1 << len(v)) - 1 for v in phases)
    scratch = [
        V((2, 4, 2, 128, D), BF),
        V((3, 4, 256, W3), BF),
        V((3, 4, 256, W3), BF),
        V((3, 4, 256, W3), BF),
        V((3, 2, 2, 2, 128, W3), BF),
        V((3, 4, 2, 128, W3), BF),
        V((3, 2, 128, D), F32),
        V((2, 3 * W3, D), BF),
        V((2, D, 1024), BF),
        V((3, W3, 1024), BF),
        V((3, 8, 1024), F32),
        V((3, W3, 1024), F32),
        V((3, 4, 256, 3 * W3), BF),
        V((2, 1, D), F32),
        V((4, 2, 128, D), BF),
        V((4, 128, D), BF),
        V((4, 2, 128, D), BF),
        V((2, 2, 128, D), BF),
        V((2, 128, D), BF),
        V((2, 128, D), BF),
        V((4, 128, D), BF),
        V((2, 128, D), BF),
        V((2, D, 3 * W3), F32),
        V((2, 2, 2, 2, 96, 256), BF),
        V((2, 2, 2, 2, 96, 256), BF),
        V((2, 2, 2, 2, 96, 64), BF),
        V((len(phases), 4, 16, D), F32),
        V((16, D), F32),
    ]
    for index in range(7):
        shapes, _ = set_shapes(index)
        scratch += [V(shape, BF) for shape in shapes[1:-1]]
        scratch += [V((ways(a) - 1,) + shapes[k + 1], BF) for k, a in enumerate(ORDERS[index])]
    scratch += [
        pltpu.SemaphoreType.DMA((56 + sums,)),
        pltpu.SemaphoreType.DMA((56 + sums,)),
        pltpu.SemaphoreType.DMA((23,)),
    ]
    return pl.pallas_call(
        functools.partial(kernel_two, n_dp),
        out_shape=[o for o, _ in outs],
        in_specs=[sm, any_, any_, vm] + [any_] * 6 + [vm] * 4,
        out_specs=[s for _, s in outs],
        scratch_shapes=scratch,
        compiler_params=pltpu.CompilerParams(
            collective_id=1, has_side_effects=True, vmem_limit_bytes=VMEM_LIMIT
        ),
    )(*args)


def kernel_three(
    block_in, tok_in, a_in, b_in, c_in, d_in, rep, eb, qv,
    block_out, tok_out, a_out, b_out, c_out, d_out, v0, v1, v2, v3, v4, v5, e_out, q_out,
):
    block_out[...] = block_in[...]
    tok_out[...] = tok_in[...]

    @pl.when(pl.program_id(0) == 0)
    def _():
        a_out[...] = a_in[...]
        b_out[...] = b_in[...]
        c_out[...] = c_in[...].T
        for j in range(3):
            d_out[j] = d_in[:, j * W3 : (j + 1) * W3]
        for k, ref in enumerate((v0, v1, v2, v3, v4, v5)):
            ref[...] = rep[k : k + 1, :].reshape(D)
        e_out[...] = eb[...].reshape(D)
        q_out[0:1, :] = qv[:, 0:W3]
        q_out[1:2, :] = qv[:, 256 : 256 + W3]


def call_three(*args):
    part = pl.BlockSpec((3, 2, 128, D), lambda i: (i, 0, 0, 0))
    vm = pl.BlockSpec(memory_space=pltpu.VMEM)
    S = jax.ShapeDtypeStruct
    outs = [S((12, 2, 128, D), BF)] * 2 + [S((96, D), F32)] * 2
    outs += [S((W3, 96), F32), S((3, 96, W3), F32)] + [S((D,), F32)] * 7 + [S((2, W3), F32)]
    return pl.pallas_call(
        kernel_three,
        out_shape=outs,
        grid=(4,),
        in_specs=[part] * 2 + [vm] * 7,
        out_specs=[part] * 2 + [vm] * 12,
        compiler_params=pltpu.CompilerParams(vmem_limit_bytes=VMEM_LIMIT),
    )(*args)


def body(
    n_dp, tokens, lengths, first_gain, first_shift, input_weight, query_value_bias, output_weight,
    output_bias, second_gain, second_shift, expand_weight, expand_bias, reduce_weight, reduce_bias,
    cotangent,
):
    tok = tokens.reshape(12, 2, 128, D)
    cot = cotangent.reshape(12, 2, 128, D)
    win = jnp.transpose(input_weight, (1, 2, 0)).reshape(3 * W3, D)
    block_out, qkv, lse, att, do, gm, winr, ab, cg, sva = call_one(
        lengths, tok, cot, win, output_weight, expand_weight, reduce_weight, first_gain, first_shift,
        output_bias, second_gain, second_shift, reduce_bias, expand_bias, query_value_bias,
    )
    found = call_two(
        n_dp, lengths, tok, qkv, lse, att, do, gm.reshape(3, 2, 2, 128, D), win, winr,
        ab.reshape(3, 2, 2, 2, 2, 2, 96, 256), cg.reshape(2, 2, 2, 2, 96, W3), sva, first_gain, first_shift,
    )
    block_out, tok_grad, a, b, cc, d, v0, v1, v2, v3, v4, v5, eb, qv = call_three(block_out, *found)
    left = n_dp // 8
    if left > 1:
        groups = [list(range(k * left, (k + 1) * left)) for k in range(8)]
        a, b, cc, d = [
            lax.psum_scatter(v, "dp", scatter_dimension=at, axis_index_groups=groups, tiled=True)
            for v, at in ((a, 0), (b, 0), (cc, 1), (d, 1))
        ]
    return (
        block_out.reshape(tokens.shape),
        tok_grad.reshape(tokens.shape),
        v0,
        v1,
        jnp.transpose(d, (1, 0, 2)),
        qv,
        cc,
        v2,
        v3,
        v4,
        a,
        eb,
        b.T,
        v5,
    )


def solution(mesh):
    return jax.shard_map(
        functools.partial(body, mesh.shape["dp"]),
        mesh=mesh,
        in_specs=(
            P("dp", None),
            P("dp"),
            P(),
            P(),
            P(None, None, "tensor"),
            P(None, "tensor"),
            P("tensor", None),
            P(),
            P(),
            P(),
            P(None, "tensor"),
            P("tensor"),
            P("tensor", None),
            P(),
            P("dp", None),
        ),
        out_specs=(
            P("dp", None),
            P("dp", None),
            P(),
            P(),
            P("dp", None, "tensor"),
            P(None, "tensor"),
            P("tensor", "dp"),
            P(),
            P(),
            P(),
            P("dp", "tensor"),
            P("tensor"),
            P("tensor", "dp"),
            P(),
        ),
        check_vma=False,
    )
```
